32 devices in a mesh: seq: 8 (over z, x), tensor: 4 (over y, core).
Axes of the slice: x: 2, y: 2, z: 4, core: 2. Of those that a mesh axis runs over, the one named last changes fastest.
Arguments:
- queries: bfloat16 [2560, 2048], P('seq', 'tensor'), may hold values from -8 to 8
- key_rows: bfloat16 [2560, 512], P('seq', 'tensor'), may hold values from -8 to 8
- value_rows: bfloat16 [2560, 512], P('seq', 'tensor'), may hold values from -6 to 6
- out_weight: bfloat16 [2048, 8192], P('tensor', 'seq'), may hold values from -0.125 to 0.125
- residual_in: bfloat16 [2560, 8192], P('seq'), may hold values from -0.1796875 to 0.1796875
- norm_gain: bfloat16 [8192], replicated, may hold values from 0.099609375 to 1.8984375
- prompt_lengths: int32 [18], replicated, may hold values from 1 to 1280, 2560 in all
Outputs:
- normed: bfloat16 [2560, 8192], P('seq')
- cache_keys: bfloat16 [5632, 512], P('seq', 'tensor')
- cache_values: bfloat16 [5632, 512], P('seq', 'tensor')
The draws below stay inside these ranges and needn't reach their ends.
Inputs may be any that keep to these rules, and one draw needn't show every extreme that they name: `prompt_lengths`: the 18 lengths sum to 2560, and the largest is 1280.
All inputs are finite; a program needn't handle non-finite values.
Results may differ from the reference program's by a relative error of at most 0.019.
Values may be sent and summed in bfloat16 or wider, within the bound.
A program may use at most 192 MiB of HBM per device.

```python
import math
import jax
import jax.numpy as jnp
import numpy as np
from jax import lax

D = 8192
HD = 128
QPK = 4
SEQS = 18
PAGE = 128
TOK_DEV = 320
TOKENS = 2560
KVH = 4
QH = 16
SLOTS = 5632
N_SEQ = 8
N_TENSOR = 4


def draw_queries(key, part):
    width = QH * HD
    result = jnp.clip(jax.random.normal(jax.random.fold_in(key, 1), (TOKENS, width), jnp.float32), -6.0, 6.0)
    return result.astype(jnp.bfloat16)


def draw_key_rows(key, part):
    width = KVH * HD
    result = jnp.clip(jax.random.normal(jax.random.fold_in(key, 2), (TOKENS, width), jnp.float32), -6.0, 6.0)
    return result.astype(jnp.bfloat16)


def level_of(own_key, shape, split, smallest, largest):
    loudness, own = 1.0, jax.random.fold_in(own_key, 6)
    for dim, blocks in split:
        steps = jnp.exp(jax.random.uniform(jax.random.fold_in(own, dim), (blocks,), jnp.float32, smallest / len(split), largest / len(split)))
        loudness = loudness * jnp.repeat(steps, shape[dim] // blocks).reshape([-1 if axis == dim else 1 for axis in range(len(shape))])
    return loudness


def split_up(amount, total, most, slope):
    weights = [(1 << 20) // math.isqrt(rank ** slope) + 1 for rank in range(2, amount + 1)]
    surplus, counts = total - most - (amount - 1), [1] * (amount - 1)
    while surplus > 0:
        candidates = [i for i in range(amount - 1) if counts[i] < most]
        mass, budget = sum([weights[i] for i in candidates]), surplus
        for i in candidates:
            more = min(most - counts[i], max(1, budget * weights[i] // mass), surplus)
            counts[i] = counts[i] + more
            surplus = surplus - more
    return np.array([most] + counts)


def uneven_parts(own_key, count, total, limit, lean):
    if count == 2:
        one = jax.random.randint(own_key, (), max(1, total - limit), min(limit, total - 1) + 1)
        return jnp.stack([one, total - one])
    sizes = jnp.asarray(split_up(count, total, limit, lean), jnp.int32)
    twos = (count - 1) // 2
    donor, taker = sizes[1:1 + 2 * twos:2], sizes[2:2 + 2 * twos:2]
    margin = jnp.minimum(donor - 1, limit - taker)
    moved = jax.random.randint(jax.random.fold_in(own_key, 1), (twos,), 0, 1 << 20) % (margin + 1)
    sizes = sizes.at[1:1 + 2 * twos:2].set(donor - moved).at[2:2 + 2 * twos:2].set(taker + moved)
    return sizes[jax.random.permutation(jax.random.fold_in(own_key, 2), count)]


def gaussian(own_key, extent, scale, bound, cuts=(), held_as=jnp.bfloat16):
    array = jax.random.normal(own_key, extent, jnp.float32) * scale
    if len(cuts) > 0:
        array = level_of(own_key, extent, cuts, -0.22, 0.18) * array
    return jnp.clip(array, min=-bound, max=bound).astype(held_as)


def setup_inputs(seed: int = 0) -> dict:
    key_of = jax.random.split(jax.random.key(seed), 8)
    return {
        "queries": draw_queries(jax.random.fold_in(key_of[7], 71), 0),
        "key_rows": draw_key_rows(jax.random.fold_in(key_of[7], 71), 0),
        "value_rows": gaussian(key_of[2], (TOKENS, KVH * HD), 1.0, 6.0, ((0, 8), (1, 4))),
        "out_weight": gaussian(key_of[3], (QH * HD, D), (QH * HD) ** -0.5, 0.125, ((0, 4), (1, 8))),
        "residual_in": gaussian(key_of[4], (TOKENS, D), 0.03, 0.1796875, ((0, 8),)),
        "norm_gain": jnp.clip(1.0 + 0.18 * jax.random.normal(key_of[5], (D,), jnp.float32), 0.099609375, 1.8984375).astype(jnp.bfloat16),
        "prompt_lengths": uneven_parts(key_of[6], SEQS, TOKENS, TOKENS // 2, 2).astype(jnp.int32),
    }


def position_of(stored, per_device, devices):
    half_block = per_device // 2
    device = stored // per_device
    offset = stored % per_device
    return jnp.where(offset < half_block, device * half_block + offset, (2 * devices - 1 - device) * half_block + offset - half_block).astype(jnp.int32)

def stored_row(position, per_device, devices):
    half_block = per_device // 2
    block_index = position // half_block
    device = jnp.where(block_index < devices, block_index, 2 * devices - 1 - block_index)
    offset = position % half_block + jnp.where(block_index < devices, 0, half_block)
    return (device * per_device + offset).astype(jnp.int32)

def segment_of(position, lengths):
    doc_ends = jnp.cumsum(lengths, dtype=jnp.int32)
    return lax.optimization_barrier(jnp.sum((position[:, None] >= doc_ends[None, :]).astype(jnp.int32), axis=1, dtype=jnp.int32))

def slot_source(slot_ids, lengths, page_size):
    padded = (lengths + page_size - 1) // page_size * page_size
    page_ends = jnp.cumsum(padded, dtype=jnp.int32)
    page_starts = page_ends - padded
    doc_ends = jnp.cumsum(lengths, dtype=jnp.int32)
    doc_starts = doc_ends - lengths
    prompt = lax.optimization_barrier(jnp.sum((slot_ids[:, None] >= page_ends[None, :]).astype(jnp.int32), axis=1, dtype=jnp.int32))
    clipped = jnp.minimum(prompt, lengths.shape[0] - 1)
    within = slot_ids - jnp.take(page_starts, clipped)
    is_live = (prompt < lengths.shape[0]) & (within < jnp.take(lengths, clipped))
    return ((jnp.take(doc_starts, clipped) + within).astype(jnp.int32), is_live)

def reference(queries, key_rows, value_rows, out_weight, residual_in, norm_gain, prompt_lengths):
    stored = jnp.arange(TOKENS, dtype=jnp.int32)
    position = position_of(stored, TOK_DEV, N_SEQ)
    segment = segment_of(position, prompt_lengths)
    score_scale = 1.0 / math.sqrt(HD)
    kv_heads = key_rows.shape[1] // HD
    key_float = key_rows.astype(jnp.float32).reshape(TOKENS, kv_heads, HD)
    value_float = value_rows.astype(jnp.float32).reshape(TOKENS, kv_heads, HD)
    query_blocks = queries.reshape(N_SEQ, TOK_DEV, kv_heads, QPK, HD)
    pos_blocks = position.reshape(N_SEQ, TOK_DEV)
    seg_blocks = segment.reshape(N_SEQ, TOK_DEV)

    def attend(block_inputs):
        query_block, query_pos, query_seg = block_inputs
        scores = jnp.einsum('qgjd,kgd->gjqk', query_block.astype(jnp.float32), key_float) * score_scale
        allowed = (position[None, :] <= query_pos[:, None]) & (segment[None, :] == query_seg[:, None])
        scores = jnp.where(allowed, scores, -1e+30)
        row_max = lax.optimization_barrier(jnp.max(scores, axis=-1, keepdims=True))
        weights = jnp.where(allowed, jnp.exp(scores - row_max), 0.0)
        totals = lax.optimization_barrier(jnp.sum(weights, axis=-1))
        rounded = lax.optimization_barrier(weights.astype(jnp.bfloat16)).astype(jnp.float32)
        summed = jnp.einsum('gjqk,kgd->qgjd', rounded, value_float)
        return (summed / jnp.transpose(totals, (2, 0, 1))[..., None]).astype(jnp.bfloat16)
    attended = lax.map(attend, (query_blocks, pos_blocks, seg_blocks)).reshape(TOKENS, -1)
    group_width = out_weight.shape[0] // N_TENSOR
    projected = jnp.zeros((TOKENS, out_weight.shape[1]), jnp.float32)
    for tensor_group in range(N_TENSOR):
        low = tensor_group * group_width
        partial_value = jnp.dot(attended[:, low:low + group_width], out_weight[low:low + group_width], preferred_element_type=jnp.float32)
        partial_value = lax.optimization_barrier(partial_value.astype(jnp.bfloat16)).astype(jnp.float32)
        projected = projected + partial_value
    hidden = residual_in.astype(jnp.float32) + projected
    mean_square = lax.optimization_barrier(jnp.mean(hidden * hidden, axis=-1, keepdims=True))
    normed = (hidden * lax.rsqrt(mean_square + 1e-05) * norm_gain.astype(jnp.float32)).astype(jnp.bfloat16)
    slot_ids = jnp.arange(SLOTS, dtype=jnp.int32)
    source, is_live = slot_source(slot_ids, prompt_lengths, PAGE)
    rows_at = jnp.clip(stored_row(source, TOK_DEV, N_SEQ), 0, TOKENS - 1).astype(jnp.int32)
    cache_keys = jnp.where(is_live[:, None], jnp.take(key_rows, rows_at, axis=0), jnp.zeros((), jnp.bfloat16))
    cache_values = jnp.where(is_live[:, None], jnp.take(value_rows, rows_at, axis=0), jnp.zeros((), jnp.bfloat16))
    return (normed, cache_keys, cache_values)
```

```python
import functools
import math

import jax
import jax.numpy as jnp
from jax import lax
from jax.experimental import pallas as pl
from jax.experimental.pallas import tpu as pltpu
from jax.sharding import PartitionSpec as P

HD = 128
PAGE = 128
SLOT_DEV = 704
LINE = 4
CORES = 2
KEYS = 256
ROW_TILE = 16
MESH = pl.DeviceIdType.MESH


def kernel(
    n_seq,
    n_tensor,
    q_ref,
    k_ref,
    v_ref,
    w_ref,
    res_ref,
    gain_ref,
    len_ref,
    normed_ref,
    ck_ref,
    cv_ref,
    kv,
    wbuf,
    att,
    prod,
    proj,
    res,
    m_ref,
    l_ref,
    acc_ref,
    kv_send,
    kv_recv,
    w_send,
    w_recv,
    w_local,
    a_send,
    a_recv,
    p_send,
    p_recv,
    res_sem,
):
    rest = n_seq // LINE
    pairs = n_tensor // CORES
    rows = q_ref.shape[0]
    half = rows // 2
    tokens = kv.shape[0]
    heads = q_ref.shape[1] // HD
    depth = w_ref.shape[0]
    width = wbuf.shape[2]
    parts = w_ref.shape[1] // width
    n_prompts = len_ref.shape[0]

    seq = lax.axis_index("seq")
    ten = lax.axis_index("tensor")
    line = seq // rest
    col = seq % rest
    pair = ten // CORES
    core = ten % CORES

    def line_peer(j):
        return ((line + j) % LINE) * rest + col

    def col_peer(i):
        return line * rest + (col + i) % rest

    def pair_peer(i):
        return ((pair + i) % pairs) * CORES + core

    twin = pair * CORES + 1 - core

    def remote(src, dst, send, recv, to_seq, to_ten):
        return pltpu.make_async_remote_copy(
            src_ref=src,
            dst_ref=dst,
            send_sem=send,
            recv_sem=recv,
            device_id=(to_seq, to_ten),
            device_id_type=MESH,
        )

    res_copy = pltpu.make_async_copy(res_ref, res, res_sem)
    res_copy.start()

    barrier = pltpu.get_barrier_semaphore()
    greeted = 0
    for j in range(1, LINE):
        pl.semaphore_signal(barrier, inc=1, device_id=(line_peer(j), ten), device_id_type=MESH)
        greeted += 1
    for i in range(rest):
        for k in range(n_tensor):
            if i == 0 and k == 0:
                continue
            pl.semaphore_signal(
                barrier,
                inc=1,
                device_id=(col_peer(i), (ten + k) % n_tensor),
                device_id_type=MESH,
            )
            greeted += 1

    def kv_rows(source, h):
        block = source if h == 0 else 2 * n_seq - 1 - source
        return pl.ds(pl.multiple_of(block * half, half), half)

    for h in range(2):
        kv[kv_rows(seq, h), :HD] = k_ref[h * half : (h + 1) * half, :]
        kv[kv_rows(seq, h), HD:] = v_ref[h * half : (h + 1) * half, :]
    pl.semaphore_wait(barrier, greeted)

    sent = []

    def kv_copy(source, h, j, i, to_seq):
        at = kv.at[kv_rows(source, h)]
        return remote(at, at, kv_send.at[j, i, h], kv_recv.at[source, h], to_seq, ten)

    def kv_start(source, h, j, i, to_seq):
        copy = kv_copy(source, h, j, i, to_seq)
        copy.start()
        sent.append(copy)

    for h in range(2):
        for j in (2, 1, 3):
            kv_start(seq, h, j, 0, line_peer(j))
    for h in range(2):
        for i in range(1, rest):
            kv_start(seq, h, 0, i, col_peer(i))
    for j in (1, 3, 2):
        source = line_peer(j)
        for h in range(2):
            kv_copy(source, h, j, 0, seq).wait_recv()
            for i in range(1, rest):
                kv_start(source, h, j, i, col_peer(i))

    mine = (col * parts <= ten) & (ten < (col + 1) * parts)
    for i in range(rest):
        for k in range(parts):
            target = col * parts + k
            piece = w_ref.at[:, pl.ds(k * width, width)]
            copy = remote(
                piece, wbuf.at[ten], w_send.at[i, k], w_recv.at[ten], col_peer(i), target
            )
            if i == 0:

                @pl.when(target != ten)
                def _(copy=copy):
                    copy.start()

                @pl.when(target == ten)
                def _(piece=piece):
                    pltpu.make_async_copy(piece, wbuf.at[ten], w_local).start()

            else:
                copy.start()

    starts = [jnp.int32(0)]
    for p in range(n_prompts - 1):
        starts.append(starts[-1] + len_ref[p])

    for i in range(1, rest):
        for j in range(LINE):
            source = ((line + j) % LINE) * rest + (col + i) % rest
            for h in range(2):
                kv_copy(source, h, j, i, seq).wait_recv()

    scale = 1.0 / math.sqrt(HD)
    for h in range(2):
        block = seq if h == 0 else 2 * n_seq - 1 - seq
        query = jnp.concatenate(
            [q_ref[h * half : (h + 1) * half, g * HD : (g + 1) * HD] for g in range(heads)], axis=0
        )
        position = block * half + lax.broadcasted_iota(jnp.int32, (half, 1), 0)
        begin = jnp.zeros((half, 1), jnp.int32)
        for p in range(1, n_prompts):
            begin = jnp.where(starts[p] <= position, starts[p], begin)
        m_ref[...] = jnp.full_like(m_ref, -1e20)
        l_ref[...] = jnp.zeros_like(l_ref)
        acc_ref[...] = jnp.zeros_like(acc_ref)

        def step(c, carry, query=query, position=position, begin=begin):
            at = pl.ds(pl.multiple_of(c * KEYS, KEYS), KEYS)
            scores = lax.dot_general(
                query,
                kv[at, :HD],
                (((1,), (1,)), ((), ())),
                preferred_element_type=jnp.float32,
            )
            where = c * KEYS + lax.broadcasted_iota(jnp.int32, (half, KEYS), 1)
            bias = jnp.where((where >= begin) & (where <= position), 0.0, -1e30)
            scores = scores * scale + jnp.concatenate([bias] * heads, axis=0)
            old = m_ref[:, :1]
            top = jnp.maximum(old, jnp.max(scores, axis=1, keepdims=True))
            shrink = jnp.exp(old - top)
            weights = jnp.exp(scores - top)
            total = l_ref[:, :1] * shrink + jnp.sum(weights, axis=1, keepdims=True)
            acc_ref[...] = acc_ref[...] * shrink + jnp.dot(
                weights.astype(jnp.bfloat16), kv[at, HD:], preferred_element_type=jnp.float32
            )
            m_ref[...] = jnp.broadcast_to(top, m_ref.shape)
            l_ref[...] = jnp.broadcast_to(total, l_ref.shape)
            return carry

        lax.fori_loop(0, ((block + 1) * half + KEYS - 1) // KEYS, step, 0)
        result = (acc_ref[...] / l_ref[...]).astype(jnp.bfloat16)
        for g in range(heads):
            att[line, ten, h * half : (h + 1) * half, g * HD : (g + 1) * HD] = result[
                g * half : (g + 1) * half
            ]

    def piece_copy(buf, send, recv, at_line, at_ten, slot, to_ten):
        at = buf.at[at_line, at_ten]
        return remote(at, at, send.at[slot], recv.at[at_line, at_ten], seq, to_ten)

    def spread(buf, send, recv, j):
        at_line = (line + j) % LINE
        for i in range(1, pairs):
            copy = piece_copy(buf, send, recv, at_line, ten, (j, i), pair_peer(i))
            copy.start()
            sent.append(copy)
        copy = piece_copy(buf, send, recv, at_line, ten, (j, pairs), twin)
        copy.start()
        sent.append(copy)

    def relay(buf, send, recv, j):
        at_line = (line + j) % LINE
        for i in range(1, pairs):
            source = pair_peer(pairs - i)
            piece_copy(buf, send, recv, at_line, source, (j, 0), ten).wait_recv()
            copy = piece_copy(buf, send, recv, at_line, source, (j, pairs + i), twin)
            copy.start()
            sent.append(copy)

    def settle(buf, send, recv, j):
        at_line = (line + j) % LINE
        for y in range(pairs):
            source = y * CORES + 1 - core
            piece_copy(buf, send, recv, at_line, source, (j, 0), ten).wait_recv()

    def arrive(buf, send, recv, j):
        at_line = (line + j) % LINE
        piece_copy(buf, send, recv, at_line, ten, (j, 0), ten).wait_recv()
        spread(buf, send, recv, j)

    for j in (2, 1, 3):
        at = att.at[line, ten]
        copy = remote(at, at, a_send.at[j, 0], a_recv.at[line, ten], line_peer(j), ten)
        copy.start()
        sent.append(copy)
    spread(att, a_send, a_recv, 0)

    slots = seq * SLOT_DEV + lax.broadcasted_iota(jnp.int32, (SLOT_DEV, 1), 0)
    source_of = jnp.full((SLOT_DEV, 1), -1, jnp.int32)
    page = jnp.int32(0)
    for p in range(n_prompts):
        length = len_ref[p]
        within = slots - page
        live = (within >= 0) & (within < length)
        source_of = jnp.where(live, within + starts[p], source_of)
        page = page + (length + PAGE - 1) // PAGE * PAGE
    picked = jnp.zeros((SLOT_DEV, 2 * HD), jnp.float32)

    def pick(c, picked):
        at = pl.ds(pl.multiple_of(c * KEYS, KEYS), KEYS)
        where = c * KEYS + lax.broadcasted_iota(jnp.int32, (SLOT_DEV, KEYS), 1)
        hot = jnp.where(where == source_of, 1.0, 0.0).astype(jnp.bfloat16)
        return picked + jnp.dot(hot, kv[at, :], preferred_element_type=jnp.float32)

    picked = lax.fori_loop(0, tokens // KEYS, pick, picked)
    ck_ref[...] = picked[:, :HD].astype(jnp.bfloat16)
    cv_ref[...] = picked[:, HD:].astype(jnp.bfloat16)

    def w_wait():
        owner = line * rest + ten // parts
        for k in range(n_tensor):

            @pl.when((owner == seq) & (ten == k))
            def _(k=k):
                pltpu.make_async_copy(
                    w_ref.at[:, pl.ds(0, width)], wbuf.at[k], w_local
                ).wait()

            @pl.when((owner != seq) | (ten != k))
            def _(k=k):
                remote(
                    w_ref.at[:, pl.ds(0, width)],
                    wbuf.at[k],
                    w_send.at[0, 0],
                    w_recv.at[k],
                    seq,
                    ten,
                ).wait_recv()

    def multiply(j):
        at_line = (line + j) % LINE
        total = jnp.zeros((rows, width), jnp.float32)

        def add(k, total):
            return total + jnp.dot(
                att[at_line, k], wbuf[k], preferred_element_type=jnp.float32
            )

        total = lax.fori_loop(0, n_tensor, add, total)
        if j == 0:
            proj[line, ten] = total.astype(jnp.bfloat16)
            spread(proj, p_send, p_recv, 0)
        else:
            prod[j] = total.astype(jnp.bfloat16)
            copy = remote(
                prod.at[j],
                proj.at[line, ten],
                p_send.at[j, 0],
                p_recv.at[line, ten],
                line_peer(j),
                ten,
            )
            copy.start()
            sent.append(copy)

    order = (0, 1, 3, 2)
    for n in range(LINE + 1):
        if n + 1 < LINE:
            arrive(att, a_send, a_recv, order[n + 1])
        if n < LINE:
            relay(att, a_send, a_recv, order[n])
        if n == 0:
            w_wait()
        if n < LINE:
            settle(att, a_send, a_recv, order[n])
            multiply(order[n])
    for n in range(1, LINE):
        arrive(proj, p_send, p_recv, order[n])
        relay(proj, p_send, p_recv, order[n - 1])
    relay(proj, p_send, p_recv, order[LINE - 1])
    res_copy.wait()
    for n in range(LINE):
        settle(proj, p_send, p_recv, order[n])

    columns = LINE * n_tensor * width

    def finish(r, carry):
        at = pl.ds(pl.multiple_of(r * ROW_TILE, ROW_TILE), ROW_TILE)
        square = jnp.zeros((ROW_TILE, width), jnp.float32)
        for a in range(LINE):
            for t in range(n_tensor):
                lo = (a * n_tensor + t) * width
                hidden = res[at, lo : lo + width].astype(jnp.float32) + proj[a, t, at, :].astype(
                    jnp.float32
                )
                square = square + hidden * hidden
        factor = lax.rsqrt(jnp.sum(square, axis=1, keepdims=True) * (1.0 / columns) + 1e-05)
        for a in range(LINE):
            for t in range(n_tensor):
                lo = (a * n_tensor + t) * width
                hidden = res[at, lo : lo + width].astype(jnp.float32) + proj[a, t, at, :].astype(
                    jnp.float32
                )
                gain = gain_ref[:, lo : lo + width].astype(jnp.float32)
                normed_ref[at, lo : lo + width] = (hidden * factor * gain).astype(jnp.bfloat16)
        return carry

    lax.fori_loop(0, rows // ROW_TILE, finish, 0)

    for copy in sent:
        copy.wait_send()
    for i in range(rest):
        for k in range(parts):
            target = col * parts + k
            copy = remote(
                w_ref.at[:, pl.ds(k * width, width)],
                wbuf.at[ten],
                w_send.at[i, k],
                w_recv.at[ten],
                col_peer(i),
                target,
            )
            if i == 0:

                @pl.when(target != ten)
                def _(copy=copy):
                    copy.wait_send()

            else:
                copy.wait_send()


def body(
    n_seq, n_tensor, queries, key_rows, value_rows, out_weight, residual_in, norm_gain, lengths
):
    rows, model = residual_in.shape
    width = model // (LINE * n_tensor)
    rest, pairs = n_seq // LINE, n_tensor // CORES
    parts = out_weight.shape[1] // width
    half = rows // 2
    stack = queries.shape[1] // HD * half
    depth = out_weight.shape[0]
    vmem = pl.BlockSpec(memory_space=pltpu.VMEM)
    hbm = pl.BlockSpec(memory_space=pl.ANY)
    dma = pltpu.SemaphoreType.DMA
    return pl.pallas_call(
        functools.partial(kernel, n_seq, n_tensor),
        out_shape=(
            jax.ShapeDtypeStruct((rows, model), jnp.bfloat16),
            jax.ShapeDtypeStruct((SLOT_DEV, HD), jnp.bfloat16),
            jax.ShapeDtypeStruct((SLOT_DEV, HD), jnp.bfloat16),
        ),
        in_specs=[vmem, vmem, vmem, hbm, hbm, vmem, pl.BlockSpec(memory_space=pltpu.SMEM)],
        out_specs=(vmem, vmem, vmem),
        scratch_shapes=[
            pltpu.VMEM((rows * n_seq, 2 * HD), jnp.bfloat16),
            pltpu.VMEM((n_tensor, depth, width), jnp.bfloat16),
            pltpu.VMEM((LINE, n_tensor, rows, depth), jnp.bfloat16),
            pltpu.VMEM((LINE, rows, width), jnp.bfloat16),
            pltpu.VMEM((LINE, n_tensor, rows, width), jnp.bfloat16),
            pltpu.VMEM((rows, model), jnp.bfloat16),
            pltpu.VMEM((stack, HD), jnp.float32),
            pltpu.VMEM((stack, HD), jnp.float32),
            pltpu.VMEM((stack, HD), jnp.float32),
            dma((LINE, rest, 2)),
            dma((n_seq, 2)),
            dma((rest, parts)),
            dma((n_tensor,)),
            dma,
            dma((LINE, 2 * pairs)),
            dma((LINE, n_tensor)),
            dma((LINE, 2 * pairs)),
            dma((LINE, n_tensor)),
            dma,
        ],
        compiler_params=pltpu.CompilerParams(
            collective_id=0, has_side_effects=True, vmem_limit_bytes=58 * 2**20
        ),
        cost_estimate=pl.CostEstimate(
            flops=5 * 10**9, bytes_accessed=14 * 10**6, transcendentals=2 * 10**6
        ),
    )(
        queries,
        key_rows,
        value_rows,
        out_weight,
        residual_in,
        norm_gain.reshape(1, model),
        lengths,
    )


def solution(mesh):
    return jax.shard_map(
        functools.partial(body, mesh.shape["seq"], mesh.shape["tensor"]),
        mesh=mesh,
        in_specs=(
            P("seq", "tensor"),
            P("seq", "tensor"),
            P("seq", "tensor"),
            P("tensor", "seq"),
            P("seq", None),
            P(),
            P(),
        ),
        out_specs=(P("seq", None), P("seq", "tensor"), P("seq", "tensor")),
        check_vma=False,
    )
```

```python
import functools
import math

import jax
import jax.numpy as jnp
from jax import lax
from jax.experimental import pallas as pl
from jax.experimental.pallas import tpu as pltpu
from jax.sharding import PartitionSpec as P

HD = 128
PAGE = 128
SLOT_DEV = 704
LINE = 4
CORES = 2
KEYS = 256
ROW_TILE = 16
MESH = pl.DeviceIdType.MESH


def kernel(
    n_seq,
    n_tensor,
    q_ref,
    k_ref,
    v_ref,
    w_ref,
    res_ref,
    gain_ref,
    len_ref,
    normed_ref,
    ck_ref,
    cv_ref,
    kv,
    wbuf,
    att,
    prod,
    proj,
    res,
    m_ref,
    l_ref,
    acc_ref,
    kv_send,
    kv_recv,
    w_send,
    w_recv,
    w_local,
    w_across,
    w_crossed,
    a_send,
    a_recv,
    p_send,
    p_recv,
    res_sem,
):
    rest = n_seq // LINE
    pairs = n_tensor // CORES
    rows = q_ref.shape[0]
    half = rows // 2
    tokens = kv.shape[0]
    heads = q_ref.shape[1] // HD
    width = wbuf.shape[3]
    parts = w_ref.shape[1] // width
    n_prompts = len_ref.shape[0]

    seq = lax.axis_index("seq")
    ten = lax.axis_index("tensor")
    line = seq % LINE
    col = seq // LINE
    pair = ten // CORES
    core = ten % CORES

    def line_peer(j):
        return col * LINE + (line + j) % LINE

    def col_peer(i):
        return ((col + i) % rest) * LINE + line

    def pair_peer(i):
        return ((pair + i) % pairs) * CORES + core

    twin = pair * CORES + 1 - core

    def remote(src, dst, send, recv, to_seq, to_ten):
        return pltpu.make_async_remote_copy(
            src_ref=src,
            dst_ref=dst,
            send_sem=send,
            recv_sem=recv,
            device_id=(to_seq, to_ten),
            device_id_type=MESH,
        )

    res_copy = pltpu.make_async_copy(res_ref, res, res_sem)
    res_copy.start()

    barrier = pltpu.get_barrier_semaphore()
    peers = [(line_peer(j), ten) for j in range(1, LINE)]
    peers += [(col_peer(i), ten) for i in range(1, rest)]
    peers += [(seq, (ten + k) % n_tensor) for k in range(1, n_tensor)]
    for peer in peers:
        pl.semaphore_signal(barrier, inc=1, device_id=peer, device_id_type=MESH)

    def kv_rows(source, h):
        block = source if h == 0 else 2 * n_seq - 1 - source
        return pl.ds(pl.multiple_of(block * half, half), half)

    for h in range(2):
        kv[kv_rows(seq, h), :HD] = k_ref[h * half : (h + 1) * half, :]
        kv[kv_rows(seq, h), HD:] = v_ref[h * half : (h + 1) * half, :]
    pl.semaphore_wait(barrier, len(peers))

    sent = []

    def kv_copy(source, h, i, j, to_seq):
        at = kv.at[kv_rows(source, h)]
        return remote(at, at, kv_send.at[i, j, h], kv_recv.at[source, h], to_seq, ten)

    def kv_start(source, h, i, j, to_seq):
        copy = kv_copy(source, h, i, j, to_seq)
        copy.start()
        sent.append(copy)

    for h in range(2):
        for i in range(1, rest):
            kv_start(seq, h, i, 0, col_peer(i))
        for j in (2, 1, 3):
            kv_start(seq, h, 0, j, line_peer(j))

    base = col // 2 * parts
    slot = col % 2
    holds = (base <= ten) & (ten < base + parts)
    always = parts == n_tensor

    def guarded(condition, action):
        if always:
            action()
        else:
            pl.when(condition)(action)

    def w_part(k):
        index = (ten + k) % parts
        piece = w_ref.at[:, pl.ds(pl.multiple_of(index * width, width), width)]
        return piece, base + index

    def w_first(k):
        piece, target = w_part(k)
        return remote(piece, wbuf.at[slot, ten], w_send.at[k], w_recv.at[ten], seq, target)

    def w_keep():
        return pltpu.make_async_copy(w_part(0)[0], wbuf.at[slot, ten], w_local)

    guarded(holds, lambda: w_keep().start())
    if not always:
        pl.when(jnp.logical_not(holds))(lambda: w_first(0).start())
    for k in range(1, parts):
        w_first(k).start()

    for i in range(1, rest):
        source = col_peer(i)
        for h in range(2):
            kv_copy(source, h, i, 0, seq).wait_recv()
            for j in (2, 1, 3):
                kv_start(source, h, i, j, line_peer(j))

    def w_second(i):
        return remote(
            wbuf.at[slot], wbuf.at[slot], w_across.at[i], w_crossed.at[slot], col_peer(i), ten
        )

    def w_relay():
        w_keep().wait()
        for k in range(1, n_tensor):
            source = (ten + k) % n_tensor
            remote(
                w_part(0)[0], wbuf.at[slot, source], w_send.at[0], w_recv.at[source], seq, ten
            ).wait_recv()
        for i in range(1, rest):
            w_second(i).start()

    guarded(holds, w_relay)

    def w_wait(u):
        owner = ten // parts * 2 + u

        @pl.when(owner != col)
        def _():
            remote(
                wbuf.at[u], wbuf.at[u], w_across.at[0], w_crossed.at[u], seq, ten
            ).wait_recv()

    starts = [jnp.int32(0)]
    for p in range(n_prompts - 1):
        starts.append(starts[-1] + len_ref[p])

    def kv_wait(h):
        for i in range(rest):
            for j in range(1, LINE):
                source = ((col + i) % rest) * LINE + (line + j) % LINE
                kv_copy(source, h, i, j, seq).wait_recv()

    def att_at(h, at_line, at_ten):
        return att.at[at_line, at_ten, pl.ds(h * half, half)]

    def proj_at(u, at_line, at_ten):
        return proj.at[u, at_line, at_ten]

    def piece_copy(where, n, send, recv, at_line, at_ten, slot, to_ten):
        at = where(n, at_line, at_ten)
        return remote(at, at, send.at[(n,) + slot], recv.at[n, at_line, at_ten], seq, to_ten)

    def spread(where, n, send, recv, j):
        at_line = (line + j) % LINE
        for i in range(1, pairs):
            copy = piece_copy(where, n, send, recv, at_line, ten, (j, i), pair_peer(i))
            copy.start()
            sent.append(copy)
        copy = piece_copy(where, n, send, recv, at_line, ten, (j, pairs), twin)
        copy.start()
        sent.append(copy)

    def relay(where, n, send, recv, j):
        at_line = (line + j) % LINE
        for i in range(1, pairs):
            source = pair_peer(pairs - i)
            piece_copy(where, n, send, recv, at_line, source, (j, 0), ten).wait_recv()
            copy = piece_copy(where, n, send, recv, at_line, source, (j, pairs + i), twin)
            copy.start()
            sent.append(copy)

    def settle(where, n, send, recv, j):
        at_line = (line + j) % LINE
        for y in range(pairs):
            source = y * CORES + 1 - core
            piece_copy(where, n, send, recv, at_line, source, (j, 0), ten).wait_recv()

    def arrive(where, n, send, recv, j):
        at_line = (line + j) % LINE
        piece_copy(where, n, send, recv, at_line, ten, (j, 0), ten).wait_recv()
        spread(where, n, send, recv, j)

    scale = 1.0 / math.sqrt(HD)
    for h in range(2):
        kv_wait(h)
        block = seq if h == 0 else 2 * n_seq - 1 - seq
        query = jnp.concatenate(
            [q_ref[h * half : (h + 1) * half, g * HD : (g + 1) * HD] for g in range(heads)], axis=0
        )
        position = block * half + lax.broadcasted_iota(jnp.int32, (half, 1), 0)
        begin = jnp.zeros((half, 1), jnp.int32)
        for p in range(1, n_prompts):
            begin = jnp.where(starts[p] <= position, starts[p], begin)
        m_ref[...] = jnp.full_like(m_ref, -1e20)
        l_ref[...] = jnp.zeros_like(l_ref)
        acc_ref[...] = jnp.zeros_like(acc_ref)

        def step(c, carry, query=query, position=position, begin=begin):
            at = pl.ds(pl.multiple_of(c * KEYS, KEYS), KEYS)
            scores = lax.dot_general(
                query,
                kv[at, :HD],
                (((1,), (1,)), ((), ())),
                preferred_element_type=jnp.float32,
            )
            where = c * KEYS + lax.broadcasted_iota(jnp.int32, (half, KEYS), 1)
            bias = jnp.where((where >= begin) & (where <= position), 0.0, -1e30)
            scores = scores * scale + jnp.concatenate([bias] * heads, axis=0)
            old = m_ref[:, :1]
            top = jnp.maximum(old, jnp.max(scores, axis=1, keepdims=True))
            shrink = jnp.exp(old - top)
            weights = jnp.exp(scores - top)
            total = l_ref[:, :1] * shrink + jnp.sum(weights, axis=1, keepdims=True)
            acc_ref[...] = acc_ref[...] * shrink + jnp.dot(
                weights.astype(jnp.bfloat16), kv[at, HD:], preferred_element_type=jnp.float32
            )
            m_ref[...] = jnp.broadcast_to(top, m_ref.shape)
            l_ref[...] = jnp.broadcast_to(total, l_ref.shape)
            return carry

        lax.fori_loop(0, ((block + 1) * half + KEYS - 1) // KEYS, step, 0)
        result = (acc_ref[...] / l_ref[...]).astype(jnp.bfloat16)
        for g in range(heads):
            att[line, ten, h * half : (h + 1) * half, g * HD : (g + 1) * HD] = result[
                g * half : (g + 1) * half
            ]
        spread(att_at, h, a_send, a_recv, 0)
        for j in (2, 1, 3):
            at = att_at(h, line, ten)
            copy = remote(
                at, at, a_send.at[h, j, 0], a_recv.at[h, line, ten], line_peer(j), ten
            )
            copy.start()
            sent.append(copy)

    slots = seq * SLOT_DEV + lax.broadcasted_iota(jnp.int32, (SLOT_DEV, 1), 0)
    source_of = jnp.full((SLOT_DEV, 1), -1, jnp.int32)
    page = jnp.int32(0)
    for p in range(n_prompts):
        length = len_ref[p]
        within = slots - page
        live = (within >= 0) & (within < length)
        source_of = jnp.where(live, within + starts[p], source_of)
        page = page + (length + PAGE - 1) // PAGE * PAGE
    picked = jnp.zeros((SLOT_DEV, 2 * HD), jnp.float32)

    def pick(c, picked):
        at = pl.ds(pl.multiple_of(c * KEYS, KEYS), KEYS)
        where = c * KEYS + lax.broadcasted_iota(jnp.int32, (SLOT_DEV, KEYS), 1)
        hot = jnp.where(where == source_of, 1.0, 0.0).astype(jnp.bfloat16)
        return picked + jnp.dot(hot, kv[at, :], preferred_element_type=jnp.float32)

    picked = lax.fori_loop(0, tokens // KEYS, pick, picked)
    ck_ref[...] = picked[:, :HD].astype(jnp.bfloat16)
    cv_ref[...] = picked[:, HD:].astype(jnp.bfloat16)

    def multiply(u, j):
        at_line = (line + j) % LINE

        def add(k, total):
            return total + jnp.dot(
                att[at_line, k], wbuf[u, k], preferred_element_type=jnp.float32
            )

        total = lax.fori_loop(0, n_tensor, add, jnp.zeros((rows, width), jnp.float32))
        if j == 0:
            proj[u, line, ten] = total.astype(jnp.bfloat16)
            spread(proj_at, u, p_send, p_recv, 0)
        else:
            prod[u, j] = total.astype(jnp.bfloat16)
            copy = remote(
                prod.at[u, j],
                proj.at[u, line, ten],
                p_send.at[u, j, 0],
                p_recv.at[u, line, ten],
                line_peer(j),
                ten,
            )
            copy.start()
            sent.append(copy)

    order = (0, 2, 1, 3)
    other = 1 - slot
    w_wait(slot)
    for n in range(LINE):
        for h in range(2):
            if n + 1 < LINE:
                arrive(att_at, h, a_send, a_recv, order[n + 1])
            relay(att_at, h, a_send, a_recv, order[n])
        for h in range(2):
            settle(att_at, h, a_send, a_recv, order[n])
        multiply(slot, order[n])
    w_wait(other)
    for u, last in ((slot, False), (other, True)):
        for n in range(LINE):
            if not last:
                multiply(other, order[n])
            if n + 1 < LINE:
                arrive(proj_at, u, p_send, p_recv, order[n + 1])
            relay(proj_at, u, p_send, p_recv, order[n])
    res_copy.wait()
    for u in (slot, other):
        for n in range(LINE):
            settle(proj_at, u, p_send, p_recv, order[n])

    columns = res.shape[1]
    places = [
        (u, a, t, (((t // parts * 2 + u) * LINE + a) * parts + t % parts) * width)
        for u in range(2)
        for a in range(LINE)
        for t in range(n_tensor)
    ]

    def finish(r, carry):
        at = pl.ds(pl.multiple_of(r * ROW_TILE, ROW_TILE), ROW_TILE)
        square = jnp.zeros((ROW_TILE, width), jnp.float32)
        for u, a, t, lo in places:
            hidden = res[at, lo : lo + width].astype(jnp.float32) + proj[u, a, t, at, :].astype(
                jnp.float32
            )
            square = square + hidden * hidden
        factor = lax.rsqrt(jnp.sum(square, axis=1, keepdims=True) * (1.0 / columns) + 1e-05)
        for u, a, t, lo in places:
            hidden = res[at, lo : lo + width].astype(jnp.float32) + proj[u, a, t, at, :].astype(
                jnp.float32
            )
            gain = gain_ref[:, lo : lo + width].astype(jnp.float32)
            normed_ref[at, lo : lo + width] = (hidden * factor * gain).astype(jnp.bfloat16)
        return carry

    lax.fori_loop(0, rows // ROW_TILE, finish, 0)

    for copy in sent:
        copy.wait_send()
    for k in range(1, parts):
        w_first(k).wait_send()
    if not always:
        pl.when(jnp.logical_not(holds))(lambda: w_first(0).wait_send())

    def w_sent():
        for i in range(1, rest):
            w_second(i).wait_send()

    guarded(holds, w_sent)


def body(
    n_seq, n_tensor, queries, key_rows, value_rows, out_weight, residual_in, norm_gain, lengths
):
    rows, model = residual_in.shape
    width = model // (LINE * n_tensor) // 2
    rest, pairs = n_seq // LINE, n_tensor // CORES
    parts = out_weight.shape[1] // width
    half = rows // 2
    stack = queries.shape[1] // HD * half
    depth = out_weight.shape[0]
    vmem = pl.BlockSpec(memory_space=pltpu.VMEM)
    hbm = pl.BlockSpec(memory_space=pl.ANY)
    dma = pltpu.SemaphoreType.DMA
    return pl.pallas_call(
        functools.partial(kernel, n_seq, n_tensor),
        out_shape=(
            jax.ShapeDtypeStruct((rows, model), jnp.bfloat16),
            jax.ShapeDtypeStruct((SLOT_DEV, HD), jnp.bfloat16),
            jax.ShapeDtypeStruct((SLOT_DEV, HD), jnp.bfloat16),
        ),
        in_specs=[vmem, vmem, vmem, hbm, hbm, vmem, pl.BlockSpec(memory_space=pltpu.SMEM)],
        out_specs=(vmem, vmem, vmem),
        scratch_shapes=[
            pltpu.VMEM((rows * n_seq, 2 * HD), jnp.bfloat16),
            pltpu.VMEM((2, n_tensor, depth, width), jnp.bfloat16),
            pltpu.VMEM((LINE, n_tensor, rows, depth), jnp.bfloat16),
            pltpu.VMEM((2, LINE, rows, width), jnp.bfloat16),
            pltpu.VMEM((2, LINE, n_tensor, rows, width), jnp.bfloat16),
            pltpu.VMEM((rows, model), jnp.bfloat16),
            pltpu.VMEM((stack, HD), jnp.float32),
            pltpu.VMEM((stack, HD), jnp.float32),
            pltpu.VMEM((stack, HD), jnp.float32),
            dma((rest, LINE, 2)),
            dma((n_seq, 2)),
            dma((parts,)),
            dma((n_tensor,)),
            dma,
            dma((rest,)),
            dma((2,)),
            dma((2, LINE, 2 * pairs)),
            dma((2, LINE, n_tensor)),
            dma((2, LINE, 2 * pairs)),
            dma((2, LINE, n_tensor)),
            dma,
        ],
        compiler_params=pltpu.CompilerParams(
            collective_id=0, has_side_effects=True, vmem_limit_bytes=58 * 2**20
        ),
        cost_estimate=pl.CostEstimate(
            flops=5 * 10**9, bytes_accessed=14 * 10**6, transcendentals=2 * 10**6
        ),
    )(
        queries,
        key_rows,
        value_rows,
        out_weight,
        residual_in,
        norm_gain.reshape(1, model),
        lengths,
    )


def solution(mesh):
    return jax.shard_map(
        functools.partial(body, mesh.shape["seq"], mesh.shape["tensor"]),
        mesh=mesh,
        in_specs=(
            P("seq", "tensor"),
            P("seq", "tensor"),
            P("seq", "tensor"),
            P("tensor", "seq"),
            P("seq", None),
            P(),
            P(),
        ),
        out_specs=(P("seq", None), P("seq", "tensor"), P("seq", "tensor")),
        check_vma=False,
    )
```

```python
import functools
import math

import jax
import jax.numpy as jnp
from jax import lax
from jax.experimental import pallas as pl
from jax.experimental.pallas import tpu as pltpu
from jax.sharding import PartitionSpec as P

HD = 128
PAGE = 128
SLOT_DEV = 704
LINE = 4
CORES = 2
KEYS = 256
ROW_TILE = 16
MESH = pl.DeviceIdType.MESH


def kernel(
    n_seq,
    n_tensor,
    q_ref,
    k_ref,
    v_ref,
    w_ref,
    res_ref,
    gain_ref,
    len_ref,
    normed_ref,
    ck_ref,
    cv_ref,
    kv,
    wbuf,
    att,
    prod,
    proj,
    res,
    m_ref,
    l_ref,
    acc_ref,
    kv_send,
    kv_recv,
    w_send,
    w_recv,
    w_local,
    w_across,
    w_crossed,
    a_send,
    a_recv,
    p_send,
    p_recv,
    res_sem,
):
    rest = n_seq // LINE
    pairs = n_tensor // CORES
    rows = q_ref.shape[0]
    half = rows // 2
    tokens = kv.shape[0]
    heads = q_ref.shape[1] // HD
    width = wbuf.shape[3]
    parts = w_ref.shape[1] // width
    n_prompts = len_ref.shape[0]

    seq = lax.axis_index("seq")
    ten = lax.axis_index("tensor")
    line = seq % LINE
    col = seq // LINE
    pair = ten // CORES
    core = ten % CORES

    def line_peer(j):
        return col * LINE + (line + j) % LINE

    def col_peer(i):
        return ((col + i) % rest) * LINE + line

    def pair_peer(i):
        return ((pair + i) % pairs) * CORES + core

    twin = pair * CORES + 1 - core

    def remote(src, dst, send, recv, to_seq, to_ten):
        return pltpu.make_async_remote_copy(
            src_ref=src,
            dst_ref=dst,
            send_sem=send,
            recv_sem=recv,
            device_id=(to_seq, to_ten),
            device_id_type=MESH,
        )

    res_copy = pltpu.make_async_copy(res_ref, res, res_sem)
    res_copy.start()

    barrier = pltpu.get_barrier_semaphore()
    peers = [(line_peer(j), ten) for j in range(1, LINE)]
    peers += [(col_peer(i), ten) for i in range(1, rest)]
    peers += [(seq, (ten + k) % n_tensor) for k in range(1, n_tensor)]
    for peer in peers:
        pl.semaphore_signal(barrier, inc=1, device_id=peer, device_id_type=MESH)

    def kv_rows(source, h):
        block = source if h == 0 else 2 * n_seq - 1 - source
        return pl.ds(pl.multiple_of(block * half, half), half)

    for h in range(2):
        kv[kv_rows(seq, h), :HD] = k_ref[h * half : (h + 1) * half, :]
        kv[kv_rows(seq, h), HD:] = v_ref[h * half : (h + 1) * half, :]
    pl.semaphore_wait(barrier, len(peers))

    sent = []

    def kv_copy(source, h, i, j, to_seq):
        at = kv.at[kv_rows(source, h)]
        return remote(at, at, kv_send.at[i, j, h], kv_recv.at[source, h], to_seq, ten)

    def kv_start(source, h, i, j, to_seq):
        copy = kv_copy(source, h, i, j, to_seq)
        copy.start()
        sent.append(copy)

    for h in range(2):
        for i in range(1, rest):
            kv_start(seq, h, i, 0, col_peer(i))
        for j in (2, 1, 3):
            kv_start(seq, h, 0, j, line_peer(j))

    base = col // 2 * parts
    slot = col % 2
    holds = (base <= ten) & (ten < base + parts)
    always = parts == n_tensor

    def guarded(condition, action):
        if always:
            action()
        else:
            pl.when(condition)(action)

    def w_part(k):
        index = (ten + k) % parts
        piece = w_ref.at[:, pl.ds(pl.multiple_of(index * width, width), width)]
        return piece, base + index

    def w_first(k):
        piece, target = w_part(k)
        return remote(piece, wbuf.at[slot, ten], w_send.at[k], w_recv.at[ten], seq, target)

    def w_keep():
        return pltpu.make_async_copy(w_part(0)[0], wbuf.at[slot, ten], w_local)

    def w_second(i, k):
        source = (ten + k) % n_tensor
        at = wbuf.at[slot, source]
        return remote(
            w_part(0)[0] if k == 0 else at,
            at,
            w_across.at[i, k],
            w_crossed.at[slot, source],
            col_peer(i),
            ten,
        )

    def w_begin():
        w_keep().start()
        for i in range(1, rest):
            w_second(i, 0).start()

    if not always:
        pl.when(jnp.logical_not(holds))(lambda: w_first(0).start())
    for k in range(1, parts):
        w_first(k).start()
    guarded(holds, w_begin)

    for i in range(1, rest):
        source = col_peer(i)
        for h in range(2):
            kv_copy(source, h, i, 0, seq).wait_recv()
            for j in (2, 1, 3):
                kv_start(source, h, i, j, line_peer(j))

    def w_relay():
        for k in range(1, n_tensor):
            source = (ten + k) % n_tensor
            remote(
                w_part(0)[0], wbuf.at[slot, source], w_send.at[0], w_recv.at[source], seq, ten
            ).wait_recv()
            for i in range(1, rest):
                w_second(i, k).start()
        w_keep().wait()

    guarded(holds, w_relay)

    def w_wait(u):
        owner = ten // parts * 2 + u

        @pl.when(owner != col)
        def _():
            for k in range(n_tensor):
                at = wbuf.at[u, k]
                remote(at, at, w_across.at[0, 0], w_crossed.at[u, k], seq, ten).wait_recv()

    starts = [jnp.int32(0)]
    for p in range(n_prompts - 1):
        starts.append(starts[-1] + len_ref[p])

    def kv_wait(h):
        for i in range(rest):
            for j in range(1, LINE):
                source = ((col + i) % rest) * LINE + (line + j) % LINE
                kv_copy(source, h, i, j, seq).wait_recv()

    def att_at(h, at_line, at_ten):
        return att.at[at_line, at_ten, pl.ds(h * half, half)]

    def proj_at(u, at_line, at_ten):
        return proj.at[u, at_line, at_ten]

    def piece_copy(where, n, send, recv, at_line, at_ten, slot, to_ten):
        at = where(n, at_line, at_ten)
        return remote(at, at, send.at[(n,) + slot], recv.at[n, at_line, at_ten], seq, to_ten)

    def spread(where, n, send, recv, j):
        at_line = (line + j) % LINE
        for i in range(1, pairs):
            copy = piece_copy(where, n, send, recv, at_line, ten, (j, i), pair_peer(i))
            copy.start()
            sent.append(copy)
        copy = piece_copy(where, n, send, recv, at_line, ten, (j, pairs), twin)
        copy.start()
        sent.append(copy)

    def relay(where, n, send, recv, j):
        at_line = (line + j) % LINE
        for i in range(1, pairs):
            source = pair_peer(pairs - i)
            piece_copy(where, n, send, recv, at_line, source, (j, 0), ten).wait_recv()
            copy = piece_copy(where, n, send, recv, at_line, source, (j, pairs + i), twin)
            copy.start()
            sent.append(copy)

    def settle(where, n, send, recv, j):
        at_line = (line + j) % LINE
        for y in range(pairs):
            source = y * CORES + 1 - core
            piece_copy(where, n, send, recv, at_line, source, (j, 0), ten).wait_recv()

    def arrive(where, n, send, recv, j):
        at_line = (line + j) % LINE
        piece_copy(where, n, send, recv, at_line, ten, (j, 0), ten).wait_recv()
        spread(where, n, send, recv, j)

    def att_copy(h, j, y, slot, to_seq, to_ten):
        at_line, at_ten = (line + j) % LINE, pair_peer(y)
        at = att_at(h, at_line, at_ten)
        return remote(
            at, at, a_send.at[(h,) + slot], a_recv.at[h, at_line, at_ten], to_seq, to_ten
        )

    def att_send(h, j, y, slot, to_seq, to_ten):
        copy = att_copy(h, j, y, slot, to_seq, to_ten)
        copy.start()
        sent.append(copy)

    def att_round(h, y):
        for j in (2, 1, 3):
            att_send(h, 0, y, (j, y), line_peer(j), ten)
        att_send(h, 0, y, (0, pairs + y), seq, twin)

    def att_arrive(h, j, y):
        att_copy(h, j, y, (0, 0), seq, ten).wait_recv()

    scale = 1.0 / math.sqrt(HD)
    for h in range(2):
        kv_wait(h)
        block = seq if h == 0 else 2 * n_seq - 1 - seq
        query = jnp.concatenate(
            [q_ref[h * half : (h + 1) * half, g * HD : (g + 1) * HD] for g in range(heads)], axis=0
        )
        position = block * half + lax.broadcasted_iota(jnp.int32, (half, 1), 0)
        begin = jnp.zeros((half, 1), jnp.int32)
        for p in range(1, n_prompts):
            begin = jnp.where(starts[p] <= position, starts[p], begin)
        m_ref[...] = jnp.full_like(m_ref, -1e20)
        l_ref[...] = jnp.zeros_like(l_ref)
        acc_ref[...] = jnp.zeros_like(acc_ref)

        def step(c, carry, query=query, position=position, begin=begin):
            at = pl.ds(pl.multiple_of(c * KEYS, KEYS), KEYS)
            scores = lax.dot_general(
                query,
                kv[at, :HD],
                (((1,), (1,)), ((), ())),
                preferred_element_type=jnp.float32,
            )
            where = c * KEYS + lax.broadcasted_iota(jnp.int32, (half, KEYS), 1)
            bias = jnp.where((where >= begin) & (where <= position), 0.0, -1e30)
            scores = scores * scale + jnp.concatenate([bias] * heads, axis=0)
            old = m_ref[:, :1]
            top = jnp.maximum(old, jnp.max(scores, axis=1, keepdims=True))
            shrink = jnp.exp(old - top)
            weights = jnp.exp(scores - top)
            total = l_ref[:, :1] * shrink + jnp.sum(weights, axis=1, keepdims=True)
            acc_ref[...] = acc_ref[...] * shrink + jnp.dot(
                weights.astype(jnp.bfloat16), kv[at, HD:], preferred_element_type=jnp.float32
            )
            m_ref[...] = jnp.broadcast_to(top, m_ref.shape)
            l_ref[...] = jnp.broadcast_to(total, l_ref.shape)
            return carry

        lax.fori_loop(0, ((block + 1) * half + KEYS - 1) // KEYS, step, 0)
        result = (acc_ref[...] / l_ref[...]).astype(jnp.bfloat16)
        for g in range(heads):
            att[line, ten, h * half : (h + 1) * half, g * HD : (g + 1) * HD] = result[
                g * half : (g + 1) * half
            ]
        for i in range(1, pairs):
            att_send(h, 0, 0, (0, i), seq, pair_peer(i))
        att_round(h, 0)

    slots = seq * SLOT_DEV + lax.broadcasted_iota(jnp.int32, (SLOT_DEV, 1), 0)
    source_of = jnp.full((SLOT_DEV, 1), -1, jnp.int32)
    page = jnp.int32(0)
    for p in range(n_prompts):
        length = len_ref[p]
        within = slots - page
        live = (within >= 0) & (within < length)
        source_of = jnp.where(live, within + starts[p], source_of)
        page = page + (length + PAGE - 1) // PAGE * PAGE
    picked = jnp.zeros((SLOT_DEV, 2 * HD), jnp.float32)

    def pick(c, picked):
        at = pl.ds(pl.multiple_of(c * KEYS, KEYS), KEYS)
        where = c * KEYS + lax.broadcasted_iota(jnp.int32, (SLOT_DEV, KEYS), 1)
        hot = jnp.where(where == source_of, 1.0, 0.0).astype(jnp.bfloat16)
        return picked + jnp.dot(hot, kv[at, :], preferred_element_type=jnp.float32)

    picked = lax.fori_loop(0, tokens // KEYS, pick, picked)
    ck_ref[...] = picked[:, :HD].astype(jnp.bfloat16)
    cv_ref[...] = picked[:, HD:].astype(jnp.bfloat16)

    def multiply(u, j):
        at_line = (line + j) % LINE

        def add(k, total):
            return total + jnp.dot(
                att[at_line, k], wbuf[u, k], preferred_element_type=jnp.float32
            )

        total = lax.fori_loop(0, n_tensor, add, jnp.zeros((rows, width), jnp.float32))
        if j == 0:
            proj[u, line, ten] = total.astype(jnp.bfloat16)
            spread(proj_at, u, p_send, p_recv, 0)
        else:
            prod[u, j] = total.astype(jnp.bfloat16)
            copy = remote(
                prod.at[u, j],
                proj.at[u, line, ten],
                p_send.at[u, j, 0],
                p_recv.at[u, line, ten],
                line_peer(j),
                ten,
            )
            copy.start()
            sent.append(copy)

    order = (0, 2, 1, 3)
    other = 1 - slot
    w_wait(slot)
    for h in range(2):
        for y in range(1, pairs):
            att_arrive(h, 0, y)
            att_round(h, y)
    for n in range(LINE):
        for h in range(2):
            for y in range(pairs):
                if n > 0:
                    att_arrive(h, order[n], y)
                    att_send(h, order[n], y, (order[n], pairs + y), seq, twin)
        for h in range(2):
            settle(att_at, h, a_send, a_recv, order[n])
        multiply(slot, order[n])
    w_wait(other)
    for u, last in ((slot, False), (other, True)):
        for n in range(LINE):
            if not last:
                multiply(other, order[n])
            if n + 1 < LINE:
                arrive(proj_at, u, p_send, p_recv, order[n + 1])
            relay(proj_at, u, p_send, p_recv, order[n])
    res_copy.wait()
    for u in (slot, other):
        for n in range(LINE):
            settle(proj_at, u, p_send, p_recv, order[n])

    columns = res.shape[1]
    places = [
        (u, a, t, (((t // parts * 2 + u) * LINE + a) * parts + t % parts) * width)
        for u in range(2)
        for a in range(LINE)
        for t in range(n_tensor)
    ]

    def finish(r, carry):
        at = pl.ds(pl.multiple_of(r * ROW_TILE, ROW_TILE), ROW_TILE)
        square = jnp.zeros((ROW_TILE, width), jnp.float32)
        for u, a, t, lo in places:
            hidden = res[at, lo : lo + width].astype(jnp.float32) + proj[u, a, t, at, :].astype(
                jnp.float32
            )
            square = square + hidden * hidden
        factor = lax.rsqrt(jnp.sum(square, axis=1, keepdims=True) * (1.0 / columns) + 1e-05)
        for u, a, t, lo in places:
            hidden = res[at, lo : lo + width].astype(jnp.float32) + proj[u, a, t, at, :].astype(
                jnp.float32
            )
            gain = gain_ref[:, lo : lo + width].astype(jnp.float32)
            normed_ref[at, lo : lo + width] = (hidden * factor * gain).astype(jnp.bfloat16)
        return carry

    lax.fori_loop(0, rows // ROW_TILE, finish, 0)

    for copy in sent:
        copy.wait_send()
    for k in range(1, parts):
        w_first(k).wait_send()
    if not always:
        pl.when(jnp.logical_not(holds))(lambda: w_first(0).wait_send())

    def w_sent():
        for i in range(1, rest):
            for k in range(n_tensor):
                w_second(i, k).wait_send()

    guarded(holds, w_sent)


def body(
    n_seq, n_tensor, queries, key_rows, value_rows, out_weight, residual_in, norm_gain, lengths
):
    rows, model = residual_in.shape
    width = model // (LINE * n_tensor) // 2
    rest, pairs = n_seq // LINE, n_tensor // CORES
    parts = out_weight.shape[1] // width
    half = rows // 2
    stack = queries.shape[1] // HD * half
    depth = out_weight.shape[0]
    vmem = pl.BlockSpec(memory_space=pltpu.VMEM)
    hbm = pl.BlockSpec(memory_space=pl.ANY)
    dma = pltpu.SemaphoreType.DMA
    return pl.pallas_call(
        functools.partial(kernel, n_seq, n_tensor),
        out_shape=(
            jax.ShapeDtypeStruct((rows, model), jnp.bfloat16),
            jax.ShapeDtypeStruct((SLOT_DEV, HD), jnp.bfloat16),
            jax.ShapeDtypeStruct((SLOT_DEV, HD), jnp.bfloat16),
        ),
        in_specs=[vmem, vmem, vmem, hbm, hbm, vmem, pl.BlockSpec(memory_space=pltpu.SMEM)],
        out_specs=(vmem, vmem, vmem),
        scratch_shapes=[
            pltpu.VMEM((rows * n_seq, 2 * HD), jnp.bfloat16),
            pltpu.VMEM((2, n_tensor, depth, width), jnp.bfloat16),
            pltpu.VMEM((LINE, n_tensor, rows, depth), jnp.bfloat16),
            pltpu.VMEM((2, LINE, rows, width), jnp.bfloat16),
            pltpu.VMEM((2, LINE, n_tensor, rows, width), jnp.bfloat16),
            pltpu.VMEM((rows, model), jnp.bfloat16),
            pltpu.VMEM((stack, HD), jnp.float32),
            pltpu.VMEM((stack, HD), jnp.float32),
            pltpu.VMEM((stack, HD), jnp.float32),
            dma((rest, LINE, 2)),
            dma((n_seq, 2)),
            dma((parts,)),
            dma((n_tensor,)),
            dma,
            dma((rest, n_tensor)),
            dma((2, n_tensor)),
            dma((2, LINE, 2 * pairs)),
            dma((2, LINE, n_tensor)),
            dma((2, LINE, 2 * pairs)),
            dma((2, LINE, n_tensor)),
            dma,
        ],
        compiler_params=pltpu.CompilerParams(
            collective_id=0, has_side_effects=True, vmem_limit_bytes=58 * 2**20
        ),
        cost_estimate=pl.CostEstimate(
            flops=5 * 10**9, bytes_accessed=14 * 10**6, transcendentals=2 * 10**6
        ),
    )(
        queries,
        key_rows,
        value_rows,
        out_weight,
        residual_in,
        norm_gain.reshape(1, model),
        lengths,
    )


def solution(mesh):
    return jax.shard_map(
        functools.partial(body, mesh.shape["seq"], mesh.shape["tensor"]),
        mesh=mesh,
        in_specs=(
            P("seq", "tensor"),
            P("seq", "tensor"),
            P("seq", "tensor"),
            P("tensor", "seq"),
            P("seq", None),
            P(),
            P(),
        ),
        out_specs=(P("seq", None), P("seq", "tensor"), P("seq", "tensor")),
        check_vma=False,
    )
```

```python
import functools
import math

import jax
import jax.numpy as jnp
from jax import lax
from jax.experimental import pallas as pl
from jax.experimental.pallas import tpu as pltpu
from jax.sharding import PartitionSpec as P

HD = 128
PAGE = 128
SLOT_DEV = 704
LINE = 4
CORES = 2
KEYS = 256
MESH = pl.DeviceIdType.MESH


def kernel(
    n_seq,
    n_tensor,
    q_ref,
    k_ref,
    v_ref,
    w_ref,
    res_ref,
    len_ref,
    out_ref,
    factor_ref,
    ck_ref,
    cv_ref,
    kv,
    wbuf,
    att,
    prod,
    proj,
    res,
    m_ref,
    l_ref,
    acc_ref,
    square,
    kv_send,
    kv_recv,
    w_send,
    w_recv,
    w_local,
    w_across,
    w_crossed,
    a_send,
    a_recv,
    p_send,
    p_recv,
    res_sem,
    out_sem,
):
    rest = n_seq // LINE
    pairs = n_tensor // CORES
    rows = q_ref.shape[0]
    half = rows // 2
    tokens = kv.shape[0]
    heads = q_ref.shape[1] // HD
    width = wbuf.shape[3]
    parts = w_ref.shape[1] // width
    n_prompts = len_ref.shape[0]

    seq = lax.axis_index("seq")
    ten = lax.axis_index("tensor")
    line = seq % LINE
    col = seq // LINE
    pair = ten // CORES
    core = ten % CORES

    def place(j):
        return (line // 2 + j // 2) % 2 * 2 + (line % 2 + j % 2) % 2

    def line_peer(j):
        return col * LINE + place(j)

    def col_peer(i):
        return ((col + i) % rest) * LINE + line

    def pair_peer(i):
        return ((pair + i) % pairs) * CORES + core

    twin = pair * CORES + 1 - core

    def remote(src, dst, send, recv, to_seq, to_ten):
        return pltpu.make_async_remote_copy(
            src_ref=src,
            dst_ref=dst,
            send_sem=send,
            recv_sem=recv,
            device_id=(to_seq, to_ten),
            device_id_type=MESH,
        )

    res_copy = pltpu.make_async_copy(res_ref, res, res_sem)
    res_copy.start()

    barrier = pltpu.get_barrier_semaphore()
    peers = [(line_peer(j), ten) for j in range(1, LINE)]
    peers += [(col_peer(i), ten) for i in range(1, rest)]
    peers += [(seq, (ten + k) % n_tensor) for k in range(1, n_tensor)]
    for peer in peers:
        pl.semaphore_signal(barrier, inc=1, device_id=peer, device_id_type=MESH)

    def kv_rows(source, h):
        block = source if h == 0 else 2 * n_seq - 1 - source
        return pl.ds(pl.multiple_of(block * half, half), half)

    for h in range(2):
        kv[kv_rows(seq, h), :HD] = k_ref[h * half : (h + 1) * half, :]
        kv[kv_rows(seq, h), HD:] = v_ref[h * half : (h + 1) * half, :]
    pl.semaphore_wait(barrier, len(peers))

    sent = []

    def kv_copy(source, h, i, j, to_seq):
        at = kv.at[kv_rows(source, h)]
        return remote(at, at, kv_send.at[i, j, h], kv_recv.at[source, h], to_seq, ten)

    def kv_start(source, h, i, j, to_seq):
        copy = kv_copy(source, h, i, j, to_seq)
        copy.start()
        sent.append(copy)

    def kv_source(i, j):
        return (col + i) % rest * LINE + place(j)

    def kv_square(i, h):
        kv_start(kv_source(i, 0), h, i, 2, line_peer(2))
        kv_start(kv_source(i, 0), h, i, 1, line_peer(1))

    for h in range(2):
        for i in range(1, rest):
            kv_start(seq, h, i, 0, col_peer(i))
        kv_square(0, h)

    base = col // 2 * parts
    slot = col % 2
    holds = (base <= ten) & (ten < base + parts)
    always = parts == n_tensor

    def guarded(condition, action):
        if always:
            action()
        else:
            pl.when(condition)(action)

    def w_part(k):
        index = (ten + k) % parts
        piece = w_ref.at[:, pl.ds(pl.multiple_of(index * width, width), width)]
        return piece, base + index

    def w_first(k):
        piece, target = w_part(k)
        return remote(piece, wbuf.at[slot, ten], w_send.at[k], w_recv.at[ten], seq, target)

    def w_keep():
        return pltpu.make_async_copy(w_part(0)[0], wbuf.at[slot, ten], w_local)

    def w_second(i, k):
        source = (ten + k) % n_tensor
        at = wbuf.at[slot, source]
        return remote(
            w_part(0)[0] if k == 0 else at,
            at,
            w_across.at[i, k],
            w_crossed.at[slot, source],
            col_peer(i),
            ten,
        )

    def w_begin():
        for i in range(1, rest):
            w_second(i, 0).start()

    if not always:
        pl.when(jnp.logical_not(holds))(lambda: w_first(0).start())
    for k in range(1, parts):
        w_first(k).start()
    guarded(holds, lambda: w_keep().start())

    def kv_arrive(i, j, h):
        kv_copy(kv_source(i, j), h, i, j, seq).wait_recv()

    def kv_relay(i, h):
        kv_arrive(i, 2, h)
        kv_start(kv_source(i, 2), h, i, 3, line_peer(1))

    for h in range(2):
        kv_relay(0, h)
        for i in range(1, rest):
            kv_arrive(i, 0, h)
            kv_square(i, h)
    for h in range(2):
        for i in range(1, rest):
            kv_relay(i, h)

    def w_relay():
        w_begin()
        for k in range(1, n_tensor):
            source = (ten + k) % n_tensor
            remote(
                w_part(0)[0], wbuf.at[slot, source], w_send.at[0], w_recv.at[source], seq, ten
            ).wait_recv()
            for i in range(1, rest):
                w_second(i, k).start()
        w_keep().wait()

    def w_wait(u):
        owner = ten // parts * 2 + u

        @pl.when(owner != col)
        def _():
            for k in range(n_tensor):
                at = wbuf.at[u, k]
                remote(at, at, w_across.at[0, 0], w_crossed.at[u, k], seq, ten).wait_recv()

    starts = [jnp.int32(0)]
    for p in range(n_prompts - 1):
        starts.append(starts[-1] + len_ref[p])

    def kv_wait(h):
        for i in range(rest):
            for j in (1, 3):
                kv_arrive(i, j, h)

    def att_at(h, at_line, at_ten):
        return att.at[at_line, at_ten, pl.ds(h * half, half)]

    def proj_at(u, at_line, at_ten):
        return proj.at[u, at_line, at_ten]

    def piece_copy(where, n, send, recv, at_line, at_ten, slot, to_ten):
        at = where(n, at_line, at_ten)
        return remote(at, at, send.at[(n,) + slot], recv.at[n, at_line, at_ten], seq, to_ten)

    def spread(where, n, send, recv, j):
        at_line = place(j)
        for i in range(1, pairs):
            copy = piece_copy(where, n, send, recv, at_line, ten, (j, i), pair_peer(i))
            copy.start()
            sent.append(copy)
        copy = piece_copy(where, n, send, recv, at_line, ten, (j, pairs), twin)
        copy.start()
        sent.append(copy)

    def relay(where, n, send, recv, j):
        at_line = place(j)
        for i in range(1, pairs):
            source = pair_peer(pairs - i)
            piece_copy(where, n, send, recv, at_line, source, (j, 0), ten).wait_recv()
            copy = piece_copy(where, n, send, recv, at_line, source, (j, pairs + i), twin)
            copy.start()
            sent.append(copy)

    def settle(where, n, send, recv, j):
        at_line = place(j)
        for y in range(pairs):
            source = y * CORES + 1 - core
            piece_copy(where, n, send, recv, at_line, source, (j, 0), ten).wait_recv()

    def arrive(where, n, send, recv, j):
        at_line = place(j)
        piece_copy(where, n, send, recv, at_line, ten, (j, 0), ten).wait_recv()
        spread(where, n, send, recv, j)

    def att_copy(h, j, y, slot, to_seq, to_ten):
        at_line, at_ten = place(j), pair_peer(y)
        at = att_at(h, at_line, at_ten)
        return remote(
            at, at, a_send.at[(h,) + slot], a_recv.at[h, at_line, at_ten], to_seq, to_ten
        )

    def att_send(h, j, y, slot, to_seq, to_ten):
        copy = att_copy(h, j, y, slot, to_seq, to_ten)
        copy.start()
        sent.append(copy)

    def att_round(h, y):
        for j in (2, 1):
            att_send(h, 0, y, (j, y), line_peer(j), ten)
        att_send(h, 0, y, (0, pairs + y), seq, twin)

    def att_arrive(h, j, y):
        att_copy(h, j, y, (0, 0), seq, ten).wait_recv()

    scale = 1.0 / math.sqrt(HD)
    for h in range(2):
        kv_wait(h)
        if h == 0:
            guarded(holds, w_relay)
        block = seq if h == 0 else 2 * n_seq - 1 - seq
        query = jnp.concatenate(
            [q_ref[h * half : (h + 1) * half, g * HD : (g + 1) * HD] for g in range(heads)], axis=0
        )
        position = block * half + lax.broadcasted_iota(jnp.int32, (half, 1), 0)
        begin = jnp.zeros((half, 1), jnp.int32)
        for p in range(1, n_prompts):
            begin = jnp.where(starts[p] <= position, starts[p], begin)
        m_ref[...] = jnp.full_like(m_ref, -1e20)
        l_ref[...] = jnp.zeros_like(l_ref)
        acc_ref[...] = jnp.zeros_like(acc_ref)

        def step(c, carry, query=query, position=position, begin=begin):
            at = pl.ds(pl.multiple_of(c * KEYS, KEYS), KEYS)
            scores = lax.dot_general(
                query,
                kv[at, :HD],
                (((1,), (1,)), ((), ())),
                preferred_element_type=jnp.float32,
            )
            where = c * KEYS + lax.broadcasted_iota(jnp.int32, (half, KEYS), 1)
            bias = jnp.where((where >= begin) & (where <= position), 0.0, -1e30)
            scores = scores * scale + jnp.concatenate([bias] * heads, axis=0)
            old = m_ref[:, :1]
            top = jnp.maximum(old, jnp.max(scores, axis=1, keepdims=True))
            shrink = jnp.exp(old - top)
            weights = jnp.exp(scores - top)
            total = l_ref[:, :1] * shrink + jnp.sum(weights, axis=1, keepdims=True)
            acc_ref[...] = acc_ref[...] * shrink + jnp.dot(
                weights.astype(jnp.bfloat16), kv[at, HD:], preferred_element_type=jnp.float32
            )
            m_ref[...] = jnp.broadcast_to(top, m_ref.shape)
            l_ref[...] = jnp.broadcast_to(total, l_ref.shape)
            return carry

        lax.fori_loop(0, ((block + 1) * half + KEYS - 1) // KEYS, step, 0)
        result = (acc_ref[...] / l_ref[...]).astype(jnp.bfloat16)
        for g in range(heads):
            att[line, ten, h * half : (h + 1) * half, g * HD : (g + 1) * HD] = result[
                g * half : (g + 1) * half
            ]
        for i in range(1, pairs):
            att_send(h, 0, 0, (0, i), seq, pair_peer(i))
        att_round(h, 0)

    slots = seq * SLOT_DEV + lax.broadcasted_iota(jnp.int32, (SLOT_DEV, 1), 0)
    source_of = jnp.full((SLOT_DEV, 1), -1, jnp.int32)
    page = jnp.int32(0)
    for p in range(n_prompts):
        length = len_ref[p]
        within = slots - page
        live = (within >= 0) & (within < length)
        source_of = jnp.where(live, within + starts[p], source_of)
        page = page + (length + PAGE - 1) // PAGE * PAGE
    picked = jnp.zeros((SLOT_DEV, 2 * HD), jnp.float32)

    def pick(c, picked):
        at = pl.ds(pl.multiple_of(c * KEYS, KEYS), KEYS)
        where = c * KEYS + lax.broadcasted_iota(jnp.int32, (SLOT_DEV, KEYS), 1)
        hot = jnp.where(where == source_of, 1.0, 0.0).astype(jnp.bfloat16)
        return picked + jnp.dot(hot, kv[at, :], preferred_element_type=jnp.float32)

    picked = lax.fori_loop(0, tokens // KEYS, pick, picked)
    ck_ref[...] = picked[:, :HD].astype(jnp.bfloat16)
    cv_ref[...] = picked[:, HD:].astype(jnp.bfloat16)

    def multiply(u, j):
        at_line = place(j)

        def add(k, total):
            return total + jnp.dot(
                att[at_line, k], wbuf[u, k], preferred_element_type=jnp.float32
            )

        total = lax.fori_loop(0, n_tensor, add, jnp.zeros((rows, width), jnp.float32))
        if j == 0:
            proj[u, line, ten] = total.astype(jnp.bfloat16)
            spread(proj_at, u, p_send, p_recv, 0)
        else:
            prod[u, j] = total.astype(jnp.bfloat16)
            copy = remote(
                prod.at[u, j],
                proj.at[u, line, ten],
                p_send.at[u, j, 0],
                p_recv.at[u, line, ten],
                line_peer(j),
                ten,
            )
            copy.start()
            sent.append(copy)

    square[...] = jnp.zeros_like(square)

    def column(u, a, t):
        place = ((t // parts * 2 + u) * LINE + a) * parts + t % parts
        return pl.ds(pl.multiple_of(place * width, width), width)

    def write(u, a, t):
        return pltpu.make_async_copy(
            proj.at[u, a, t], out_ref.at[:, column(u, a, t)], out_sem.at[u, a, t]
        )

    def collect(u, j):
        settle(proj_at, u, p_send, p_recv, j)
        at_line = place(j)

        def add(t, carry):
            write(u, at_line, t).start()
            hidden = res[:, column(u, at_line, t)].astype(jnp.float32) + proj[
                u, at_line, t
            ].astype(jnp.float32)
            power = hidden * hidden
            for part in range(width // HD):
                square[...] += power[:, part * HD : (part + 1) * HD]
            return carry

        lax.fori_loop(0, n_tensor, add, 0)

    order = (0, 2, 1, 3)
    other = 1 - slot
    w_wait(slot)
    for h in range(2):
        for y in range(1, pairs):
            att_arrive(h, 0, y)
            att_round(h, y)
    for n in range(LINE):
        for h in range(2):
            for y in range(pairs):
                if n > 0:
                    att_arrive(h, order[n], y)
                    if order[n] == 2:
                        att_send(h, 2, y, (3, y), line_peer(1), ten)
                    att_send(h, order[n], y, (order[n], pairs + y), seq, twin)
        for h in range(2):
            settle(att_at, h, a_send, a_recv, order[n])
        multiply(slot, order[n])
    w_wait(other)
    res_copy.wait()
    for u, last in ((slot, False), (other, True)):
        for n in range(LINE):
            if not last:
                multiply(other, order[n])
            if n + 1 < LINE:
                arrive(proj_at, u, p_send, p_recv, order[n + 1])
            relay(proj_at, u, p_send, p_recv, order[n])
            if not last and n > 0:
                collect(u, order[n - 1])
            if last and n == 0:
                collect(slot, order[LINE - 1])
    for n in range(LINE):
        collect(other, order[n])
    total = jnp.sum(square[...], axis=1, keepdims=True)
    factor = lax.rsqrt(total * (1.0 / res.shape[1]) + 1e-05)
    factor_ref[...] = jnp.broadcast_to(factor, factor_ref.shape)
    for u in range(2):
        for a in range(LINE):
            for t in range(n_tensor):
                write(u, a, t).wait()

    for copy in sent:
        copy.wait_send()
    for k in range(1, parts):
        w_first(k).wait_send()
    if not always:
        pl.when(jnp.logical_not(holds))(lambda: w_first(0).wait_send())

    def w_sent():
        for i in range(1, rest):
            for k in range(n_tensor):
                w_second(i, k).wait_send()

    guarded(holds, w_sent)


def body(
    n_seq, n_tensor, queries, key_rows, value_rows, out_weight, residual_in, norm_gain, lengths
):
    rows, model = residual_in.shape
    width = model // (LINE * n_tensor) // 2
    rest, pairs = n_seq // LINE, n_tensor // CORES
    parts = out_weight.shape[1] // width
    half = rows // 2
    stack = queries.shape[1] // HD * half
    depth = out_weight.shape[0]
    vmem = pl.BlockSpec(memory_space=pltpu.VMEM)
    hbm = pl.BlockSpec(memory_space=pl.ANY)
    dma = pltpu.SemaphoreType.DMA
    projected, factor, cache_keys, cache_values = pl.pallas_call(
        functools.partial(kernel, n_seq, n_tensor),
        out_shape=(
            jax.ShapeDtypeStruct((rows, model), jnp.bfloat16),
            jax.ShapeDtypeStruct((rows, HD), jnp.float32),
            jax.ShapeDtypeStruct((SLOT_DEV, HD), jnp.bfloat16),
            jax.ShapeDtypeStruct((SLOT_DEV, HD), jnp.bfloat16),
        ),
        in_specs=[vmem, vmem, vmem, hbm, hbm, pl.BlockSpec(memory_space=pltpu.SMEM)],
        out_specs=(hbm, vmem, vmem, vmem),
        scratch_shapes=[
            pltpu.VMEM((rows * n_seq, 2 * HD), jnp.bfloat16),
            pltpu.VMEM((2, n_tensor, depth, width), jnp.bfloat16),
            pltpu.VMEM((LINE, n_tensor, rows, depth), jnp.bfloat16),
            pltpu.VMEM((2, LINE, rows, width), jnp.bfloat16),
            pltpu.VMEM((2, LINE, n_tensor, rows, width), jnp.bfloat16),
            pltpu.VMEM((rows, model), jnp.bfloat16),
            pltpu.VMEM((stack, HD), jnp.float32),
            pltpu.VMEM((stack, HD), jnp.float32),
            pltpu.VMEM((stack, HD), jnp.float32),
            pltpu.VMEM((rows, HD), jnp.float32),
            dma((rest, LINE, 2)),
            dma((n_seq, 2)),
            dma((parts,)),
            dma((n_tensor,)),
            dma,
            dma((rest, n_tensor)),
            dma((2, n_tensor)),
            dma((2, LINE, 2 * pairs)),
            dma((2, LINE, n_tensor)),
            dma((2, LINE, 2 * pairs)),
            dma((2, LINE, n_tensor)),
            dma,
            dma((2, LINE, n_tensor)),
        ],
        compiler_params=pltpu.CompilerParams(
            collective_id=0, has_side_effects=True, vmem_limit_bytes=58 * 2**20
        ),
        cost_estimate=pl.CostEstimate(
            flops=5 * 10**9, bytes_accessed=14 * 10**6, transcendentals=2 * 10**6
        ),
    )(
        queries,
        key_rows,
        value_rows,
        out_weight,
        residual_in,
        lengths,
    )
    hidden = residual_in.astype(jnp.float32) + projected.astype(jnp.float32)
    normed = hidden * factor[:, :1] * norm_gain.astype(jnp.float32)
    return normed.astype(jnp.bfloat16), cache_keys, cache_values


def solution(mesh):
    return jax.shard_map(
        functools.partial(body, mesh.shape["seq"], mesh.shape["tensor"]),
        mesh=mesh,
        in_specs=(
            P("seq", "tensor"),
            P("seq", "tensor"),
            P("seq", "tensor"),
            P("tensor", "seq"),
            P("seq", None),
            P(),
            P(),
        ),
        out_specs=(P("seq", None), P("seq", "tensor"), P("seq", "tensor")),
        check_vma=False,
    )
```

```python
import functools
import math

import jax
import jax.numpy as jnp
from jax import lax
from jax.experimental import pallas as pl
from jax.experimental.pallas import tpu as pltpu
from jax.sharding import PartitionSpec as P

HD = 128
PAGE = 128
SLOT_DEV = 704
LINE = 4
CORES = 2
KEYS = 256
MESH = pl.DeviceIdType.MESH


def kernel(
    n_seq,
    n_tensor,
    q_ref,
    k_ref,
    v_ref,
    w_ref,
    res_ref,
    len_ref,
    out_ref,
    factor_ref,
    ck_ref,
    cv_ref,
    kv,
    wbuf,
    att,
    prod,
    proj,
    res,
    m_ref,
    l_ref,
    acc_ref,
    square,
    kv_send,
    kv_recv,
    w_send,
    w_recv,
    w_local,
    w_across,
    w_crossed,
    a_send,
    a_recv,
    p_send,
    p_recv,
    res_sem,
    out_sem,
):
    rest = n_seq // LINE
    pairs = n_tensor // CORES
    rows = q_ref.shape[0]
    half = rows // 2
    tokens = kv.shape[0]
    heads = q_ref.shape[1] // HD
    width = wbuf.shape[3]
    parts = w_ref.shape[1] // width
    n_prompts = len_ref.shape[0]

    seq = lax.axis_index("seq")
    ten = lax.axis_index("tensor")
    line = seq % LINE
    col = seq // LINE
    pair = ten // CORES
    core = ten % CORES

    def place(j):
        return (line // 2 + j // 2) % 2 * 2 + (line % 2 + j % 2) % 2

    def line_peer(j):
        return col * LINE + place(j)

    def col_peer(i):
        return ((col + i) % rest) * LINE + line

    def pair_peer(i):
        return ((pair + i) % pairs) * CORES + core

    twin = pair * CORES + 1 - core

    def remote(src, dst, send, recv, to_seq, to_ten):
        return pltpu.make_async_remote_copy(
            src_ref=src,
            dst_ref=dst,
            send_sem=send,
            recv_sem=recv,
            device_id=(to_seq, to_ten),
            device_id_type=MESH,
        )

    res_copy = pltpu.make_async_copy(res_ref, res, res_sem)
    res_copy.start()

    barrier = pltpu.get_barrier_semaphore()
    peers = [(line_peer(j), ten) for j in range(1, LINE)]
    peers += [(col_peer(i), ten) for i in range(1, rest)]
    peers += [(seq, (ten + k) % n_tensor) for k in range(1, n_tensor)]
    for peer in peers:
        pl.semaphore_signal(barrier, inc=1, device_id=peer, device_id_type=MESH)

    def kv_rows(source, h):
        block = source if h == 0 else 2 * n_seq - 1 - source
        return pl.ds(pl.multiple_of(block * half, half), half)

    for h in range(2):
        kv[kv_rows(seq, h), :HD] = k_ref[h * half : (h + 1) * half, :]
        kv[kv_rows(seq, h), HD:] = v_ref[h * half : (h + 1) * half, :]
    pl.semaphore_wait(barrier, len(peers))

    sent = []

    def kv_copy(source, h, i, j, to_seq):
        at = kv.at[kv_rows(source, h)]
        return remote(at, at, kv_send.at[i, j, h], kv_recv.at[source, h], to_seq, ten)

    def kv_start(source, h, i, j, to_seq):
        copy = kv_copy(source, h, i, j, to_seq)
        copy.start()
        sent.append(copy)

    def kv_source(i, j):
        return (col + i) % rest * LINE + place(j)

    def kv_square(i, h):
        kv_start(kv_source(i, 0), h, i, 2, line_peer(2))
        kv_start(kv_source(i, 0), h, i, 1, line_peer(1))

    for h in range(2):
        for i in range(1, rest):
            kv_start(seq, h, i, 0, col_peer(i))
        kv_square(0, h)

    base = col // 2 * parts
    slot = col % 2
    holds = (base <= ten) & (ten < base + parts)
    always = parts == n_tensor

    def guarded(condition, action):
        if always:
            action()
        else:
            pl.when(condition)(action)

    def w_part(k):
        index = (ten + k) % parts
        piece = w_ref.at[:, pl.ds(pl.multiple_of(index * width, width), width)]
        return piece, base + index

    def w_first(k):
        piece, target = w_part(k)
        return remote(piece, wbuf.at[slot, ten], w_send.at[k], w_recv.at[ten], seq, target)

    def w_keep():
        return pltpu.make_async_copy(w_part(0)[0], wbuf.at[slot, ten], w_local)

    def w_second(i, k):
        source = (ten + k) % n_tensor
        at = wbuf.at[slot, source]
        return remote(
            w_part(0)[0] if k == 0 else at,
            at,
            w_across.at[i, k],
            w_crossed.at[slot, source],
            col_peer(i),
            ten,
        )

    def w_begin():
        w_keep().start()
        for i in range(1, rest):
            w_second(i, 0).start()

    if not always:
        pl.when(jnp.logical_not(holds))(lambda: w_first(0).start())
    for k in range(1, parts):
        w_first(k).start()
    guarded(holds, w_begin)

    def kv_arrive(i, j, h):
        kv_copy(kv_source(i, j), h, i, j, seq).wait_recv()

    def kv_relay(i, h):
        kv_arrive(i, 2, h)
        kv_start(kv_source(i, 2), h, i, 3, line_peer(1))

    for h in range(2):
        kv_relay(0, h)
        for i in range(1, rest):
            kv_arrive(i, 0, h)
            kv_square(i, h)
    for h in range(2):
        for i in range(1, rest):
            kv_relay(i, h)

    def w_relay():
        for k in range(1, n_tensor):
            source = (ten + k) % n_tensor
            remote(
                w_part(0)[0], wbuf.at[slot, source], w_send.at[0], w_recv.at[source], seq, ten
            ).wait_recv()
            for i in range(1, rest):
                w_second(i, k).start()
        w_keep().wait()

    guarded(holds, w_relay)

    def w_wait(u):
        owner = ten // parts * 2 + u

        @pl.when(owner != col)
        def _():
            for k in range(n_tensor):
                at = wbuf.at[u, k]
                remote(at, at, w_across.at[0, 0], w_crossed.at[u, k], seq, ten).wait_recv()

    starts = [jnp.int32(0)]
    for p in range(n_prompts - 1):
        starts.append(starts[-1] + len_ref[p])

    def kv_wait(h):
        for i in range(rest):
            for j in (1, 3):
                kv_arrive(i, j, h)

    def att_at(h, at_line, at_ten):
        return att.at[at_line, at_ten, pl.ds(h * half, half)]

    def proj_at(u, at_line, at_ten):
        return proj.at[u, at_line, at_ten]

    def piece_copy(where, n, send, recv, at_line, at_ten, slot, to_ten):
        at = where(n, at_line, at_ten)
        return remote(at, at, send.at[(n,) + slot], recv.at[n, at_line, at_ten], seq, to_ten)

    def spread(where, n, send, recv, j):
        at_line = place(j)
        for i in range(1, pairs):
            copy = piece_copy(where, n, send, recv, at_line, ten, (j, i), pair_peer(i))
            copy.start()
            sent.append(copy)
        copy = piece_copy(where, n, send, recv, at_line, ten, (j, pairs), twin)
        copy.start()
        sent.append(copy)

    def relay(where, n, send, recv, j):
        at_line = place(j)
        for i in range(1, pairs):
            source = pair_peer(pairs - i)
            piece_copy(where, n, send, recv, at_line, source, (j, 0), ten).wait_recv()
            copy = piece_copy(where, n, send, recv, at_line, source, (j, pairs + i), twin)
            copy.start()
            sent.append(copy)

    def settle(where, n, send, recv, j):
        at_line = place(j)
        for y in range(pairs):
            source = y * CORES + 1 - core
            piece_copy(where, n, send, recv, at_line, source, (j, 0), ten).wait_recv()

    def arrive(where, n, send, recv, j):
        at_line = place(j)
        piece_copy(where, n, send, recv, at_line, ten, (j, 0), ten).wait_recv()
        spread(where, n, send, recv, j)

    def att_copy(h, j, y, slot, to_seq, to_ten):
        at_line, at_ten = place(j), pair_peer(y)
        at = att_at(h, at_line, at_ten)
        return remote(
            at, at, a_send.at[(h,) + slot], a_recv.at[h, at_line, at_ten], to_seq, to_ten
        )

    def att_send(h, j, y, slot, to_seq, to_ten):
        copy = att_copy(h, j, y, slot, to_seq, to_ten)
        copy.start()
        sent.append(copy)

    def att_round(h, y):
        for j in (2, 1):
            att_send(h, 0, y, (j, y), line_peer(j), ten)
        att_send(h, 0, y, (0, pairs + y), seq, twin)

    def att_arrive(h, j, y):
        att_copy(h, j, y, (0, 0), seq, ten).wait_recv()

    scale = math.log2(math.e) / math.sqrt(HD)
    for h in range(2):
        kv_wait(h)
        block = seq if h == 0 else 2 * n_seq - 1 - seq
        position = block * half + lax.broadcasted_iota(jnp.int32, (half, 1), 0)
        begin = jnp.zeros((half, 1), jnp.int32)
        for p in range(1, n_prompts):
            begin = jnp.where(starts[p] <= position, starts[p], begin)
        m_ref[...] = jnp.full_like(m_ref, -1e20)
        l_ref[...] = jnp.zeros_like(l_ref)
        acc_ref[...] = jnp.zeros_like(acc_ref)

        def step(c, carry, h=h, position=position, begin=begin):
            at = pl.ds(pl.multiple_of(c * KEYS, KEYS), KEYS)
            where = c * KEYS + lax.broadcasted_iota(jnp.int32, (half, KEYS), 1)
            bias = jnp.where((where >= begin) & (where <= position), 0.0, -1e30)
            for g in range(heads):
                scores = lax.dot_general(
                    q_ref[h * half : (h + 1) * half, g * HD : (g + 1) * HD],
                    kv[at, :HD],
                    (((1,), (1,)), ((), ())),
                    preferred_element_type=jnp.float32,
                )
                scores = scores * scale + bias
                old = m_ref[g]
                top = jnp.maximum(old, jnp.max(scores, axis=1, keepdims=True))
                shrink = jnp.exp2(old - top)
                weights = jnp.exp2(scores - jnp.concatenate([top] * (KEYS // HD), axis=1))
                l_ref[g] = l_ref[g] * shrink + jnp.sum(weights, axis=1, keepdims=True)
                acc_ref[g] = acc_ref[g] * shrink + jnp.dot(
                    weights.astype(jnp.bfloat16), kv[at, HD:], preferred_element_type=jnp.float32
                )
                m_ref[g] = top
            return carry

        lax.fori_loop(0, ((block + 1) * half + KEYS - 1) // KEYS, step, 0)
        for g in range(heads):
            att[line, ten, h * half : (h + 1) * half, g * HD : (g + 1) * HD] = (
                acc_ref[g] / l_ref[g]
            ).astype(jnp.bfloat16)
        for i in range(1, pairs):
            att_send(h, 0, 0, (0, i), seq, pair_peer(i))
        att_round(h, 0)

    def multiply(u, j):
        at_line = place(j)

        def add(k, total):
            return total + jnp.dot(
                att[at_line, k], wbuf[u, k], preferred_element_type=jnp.float32
            )

        total = lax.fori_loop(0, n_tensor, add, jnp.zeros((rows, width), jnp.float32))
        if j == 0:
            proj[u, line, ten] = total.astype(jnp.bfloat16)
            spread(proj_at, u, p_send, p_recv, 0)
        else:
            prod[u, j] = total.astype(jnp.bfloat16)
            copy = remote(
                prod.at[u, j],
                proj.at[u, line, ten],
                p_send.at[u, j, 0],
                p_recv.at[u, line, ten],
                line_peer(j),
                ten,
            )
            copy.start()
            sent.append(copy)

    square[...] = jnp.zeros_like(square)

    def column(u, a, t):
        place = ((t // parts * 2 + u) * LINE + a) * parts + t % parts
        return pl.ds(pl.multiple_of(place * width, width), width)

    def write(u, a, t):
        return pltpu.make_async_copy(
            proj.at[u, a, t], out_ref.at[:, column(u, a, t)], out_sem.at[u, a, t]
        )

    def collect(u, j):
        settle(proj_at, u, p_send, p_recv, j)
        at_line = place(j)

        def add(t, carry):
            write(u, at_line, t).start()
            hidden = res[:, column(u, at_line, t)].astype(jnp.float32) + proj[
                u, at_line, t
            ].astype(jnp.float32)
            power = hidden * hidden
            for part in range(width // HD):
                square[...] += power[:, part * HD : (part + 1) * HD]
            return carry

        lax.fori_loop(0, n_tensor, add, 0)

    order = (0, 2, 1, 3)
    other = 1 - slot
    w_wait(slot)
    for h in range(2):
        for y in range(1, pairs):
            att_arrive(h, 0, y)
            att_round(h, y)
    for n in range(LINE):
        for h in range(2):
            for y in range(pairs):
                if n > 0:
                    att_arrive(h, order[n], y)
                    if order[n] == 2:
                        att_send(h, 2, y, (3, y), line_peer(1), ten)
                    att_send(h, order[n], y, (order[n], pairs + y), seq, twin)
        for h in range(2):
            settle(att_at, h, a_send, a_recv, order[n])
        multiply(slot, order[n])
    slots = seq * SLOT_DEV + lax.broadcasted_iota(jnp.int32, (SLOT_DEV, 1), 0)
    source_of = jnp.full((SLOT_DEV, 1), -1, jnp.int32)
    page = jnp.int32(0)
    for p in range(n_prompts):
        length = len_ref[p]
        within = slots - page
        live = (within >= 0) & (within < length)
        source_of = jnp.where(live, within + starts[p], source_of)
        page = page + (length + PAGE - 1) // PAGE * PAGE
    picked = jnp.zeros((SLOT_DEV, 2 * HD), jnp.float32)

    def pick(c, picked):
        at = pl.ds(pl.multiple_of(c * KEYS, KEYS), KEYS)
        where = c * KEYS + lax.broadcasted_iota(jnp.int32, (SLOT_DEV, KEYS), 1)
        hot = jnp.where(where == source_of, 1.0, 0.0).astype(jnp.bfloat16)
        return picked + jnp.dot(hot, kv[at, :], preferred_element_type=jnp.float32)

    picked = lax.fori_loop(0, tokens // KEYS, pick, picked)
    ck_ref[...] = picked[:, :HD].astype(jnp.bfloat16)
    cv_ref[...] = picked[:, HD:].astype(jnp.bfloat16)

    w_wait(other)
    res_copy.wait()
    for u, last in ((slot, False), (other, True)):
        for n in range(LINE):
            if not last:
                multiply(other, order[n])
            if n + 1 < LINE:
                arrive(proj_at, u, p_send, p_recv, order[n + 1])
            relay(proj_at, u, p_send, p_recv, order[n])
            if not last and n > 0:
                collect(u, order[n - 1])
            if last and n == 0:
                collect(slot, order[LINE - 1])
    for n in range(LINE):
        collect(other, order[n])
    total = jnp.sum(square[...], axis=1, keepdims=True)
    factor = lax.rsqrt(total * (1.0 / res.shape[1]) + 1e-05)
    factor_ref[...] = jnp.broadcast_to(factor, factor_ref.shape)
    for u in range(2):
        for a in range(LINE):
            for t in range(n_tensor):
                write(u, a, t).wait()

    for copy in sent:
        copy.wait_send()
    for k in range(1, parts):
        w_first(k).wait_send()
    if not always:
        pl.when(jnp.logical_not(holds))(lambda: w_first(0).wait_send())

    def w_sent():
        for i in range(1, rest):
            for k in range(n_tensor):
                w_second(i, k).wait_send()

    guarded(holds, w_sent)


def body(
    n_seq, n_tensor, queries, key_rows, value_rows, out_weight, residual_in, norm_gain, lengths
):
    rows, model = residual_in.shape
    width = model // (LINE * n_tensor) // 2
    rest, pairs = n_seq // LINE, n_tensor // CORES
    parts = out_weight.shape[1] // width
    half = rows // 2
    heads = queries.shape[1] // HD
    depth = out_weight.shape[0]
    vmem = pl.BlockSpec(memory_space=pltpu.VMEM)
    hbm = pl.BlockSpec(memory_space=pl.ANY)
    dma = pltpu.SemaphoreType.DMA
    projected, factor, cache_keys, cache_values = pl.pallas_call(
        functools.partial(kernel, n_seq, n_tensor),
        out_shape=(
            jax.ShapeDtypeStruct((rows, model), jnp.bfloat16),
            jax.ShapeDtypeStruct((rows, HD), jnp.float32),
            jax.ShapeDtypeStruct((SLOT_DEV, HD), jnp.bfloat16),
            jax.ShapeDtypeStruct((SLOT_DEV, HD), jnp.bfloat16),
        ),
        in_specs=[vmem, vmem, vmem, hbm, hbm, pl.BlockSpec(memory_space=pltpu.SMEM)],
        out_specs=(hbm, vmem, vmem, vmem),
        scratch_shapes=[
            pltpu.VMEM((rows * n_seq, 2 * HD), jnp.bfloat16),
            pltpu.VMEM((2, n_tensor, depth, width), jnp.bfloat16),
            pltpu.VMEM((LINE, n_tensor, rows, depth), jnp.bfloat16),
            pltpu.VMEM((2, LINE, rows, width), jnp.bfloat16),
            pltpu.VMEM((2, LINE, n_tensor, rows, width), jnp.bfloat16),
            pltpu.VMEM((rows, model), jnp.bfloat16),
            pltpu.VMEM((heads, half, HD), jnp.float32),
            pltpu.VMEM((heads, half, HD), jnp.float32),
            pltpu.VMEM((heads, half, HD), jnp.float32),
            pltpu.VMEM((rows, HD), jnp.float32),
            dma((rest, LINE, 2)),
            dma((n_seq, 2)),
            dma((parts,)),
            dma((n_tensor,)),
            dma,
            dma((rest, n_tensor)),
            dma((2, n_tensor)),
            dma((2, LINE, 2 * pairs)),
            dma((2, LINE, n_tensor)),
            dma((2, LINE, 2 * pairs)),
            dma((2, LINE, n_tensor)),
            dma,
            dma((2, LINE, n_tensor)),
        ],
        compiler_params=pltpu.CompilerParams(
            collective_id=0, has_side_effects=True, vmem_limit_bytes=58 * 2**20
        ),
        cost_estimate=pl.CostEstimate(
            flops=5 * 10**9, bytes_accessed=14 * 10**6, transcendentals=2 * 10**6
        ),
    )(
        queries,
        key_rows,
        value_rows,
        out_weight,
        residual_in,
        lengths,
    )
    hidden = residual_in.astype(jnp.float32) + projected.astype(jnp.float32)
    normed = hidden * factor[:, :1] * norm_gain.astype(jnp.float32)
    return normed.astype(jnp.bfloat16), cache_keys, cache_values


def solution(mesh):
    return jax.shard_map(
        functools.partial(body, mesh.shape["seq"], mesh.shape["tensor"]),
        mesh=mesh,
        in_specs=(
            P("seq", "tensor"),
            P("seq", "tensor"),
            P("seq", "tensor"),
            P("tensor", "seq"),
            P("seq", None),
            P(),
            P(),
        ),
        out_specs=(P("seq", None), P("seq", "tensor"), P("seq", "tensor")),
        check_vma=False,
    )
```

```python
import functools
import math

import jax
import jax.numpy as jnp
from jax import lax
from jax.experimental import pallas as pl
from jax.experimental.pallas import tpu as pltpu
from jax.sharding import PartitionSpec as P

HD = 128
PAGE = 128
SLOT_DEV = 704
LINE = 4
CORES = 2
KEYS = 256
MESH = pl.DeviceIdType.MESH


def kernel(
    n_seq,
    n_tensor,
    q_ref,
    k_ref,
    v_ref,
    w_ref,
    res_ref,
    len_ref,
    out_ref,
    factor_ref,
    ck_ref,
    cv_ref,
    kv,
    wbuf,
    att,
    prod,
    proj,
    res,
    m_ref,
    l_ref,
    acc_ref,
    square,
    kv_send,
    kv_recv,
    w_send,
    w_recv,
    w_local,
    w_across,
    w_crossed,
    a_send,
    a_recv,
    p_send,
    p_recv,
    res_sem,
    out_sem,
):
    rest = n_seq // LINE
    pairs = n_tensor // CORES
    rows = q_ref.shape[0]
    half = rows // 2
    tokens = kv.shape[0]
    heads = q_ref.shape[1] // HD
    width = wbuf.shape[3]
    parts = w_ref.shape[1] // width
    n_prompts = len_ref.shape[0]

    seq = lax.axis_index("seq")
    ten = lax.axis_index("tensor")
    line = seq % LINE
    col = seq // LINE
    pair = ten // CORES
    core = ten % CORES

    def place(j):
        return (line // 2 + j // 2) % 2 * 2 + (line % 2 + j % 2) % 2

    def line_peer(j):
        return col * LINE + place(j)

    def col_peer(i):
        return ((col + i) % rest) * LINE + line

    def pair_peer(i):
        return ((pair + i) % pairs) * CORES + core

    twin = pair * CORES + 1 - core

    def remote(src, dst, send, recv, to_seq, to_ten):
        return pltpu.make_async_remote_copy(
            src_ref=src,
            dst_ref=dst,
            send_sem=send,
            recv_sem=recv,
            device_id=(to_seq, to_ten),
            device_id_type=MESH,
        )

    res_copy = pltpu.make_async_copy(res_ref, res, res_sem)
    res_copy.start()

    barrier = pltpu.get_barrier_semaphore()
    peers = [(line_peer(j), ten) for j in range(1, LINE)]
    peers += [(col_peer(i), ten) for i in range(1, rest)]
    peers += [(seq, (ten + k) % n_tensor) for k in range(1, n_tensor)]
    for peer in peers:
        pl.semaphore_signal(barrier, inc=1, device_id=peer, device_id_type=MESH)

    def kv_rows(source, h):
        block = source if h == 0 else 2 * n_seq - 1 - source
        return pl.ds(pl.multiple_of(block * half, half), half)

    for h in range(2):
        kv[kv_rows(seq, h), :HD] = k_ref[h * half : (h + 1) * half, :]
        kv[kv_rows(seq, h), HD:] = v_ref[h * half : (h + 1) * half, :]
    pl.semaphore_wait(barrier, len(peers))

    sent = []

    def kv_copy(source, h, i, j, to_seq):
        at = kv.at[kv_rows(source, h)]
        return remote(at, at, kv_send.at[i, j, h], kv_recv.at[source, h], to_seq, ten)

    def kv_start(source, h, i, j, to_seq):
        copy = kv_copy(source, h, i, j, to_seq)
        copy.start()
        sent.append(copy)

    def kv_source(i, j):
        return (col + i) % rest * LINE + place(j)

    def kv_square(i, h):
        kv_start(kv_source(i, 0), h, i, 2, line_peer(2))
        kv_start(kv_source(i, 0), h, i, 1, line_peer(1))

    for h in range(2):
        for i in range(1, rest):
            kv_start(seq, h, i, 0, col_peer(i))
        kv_square(0, h)

    base = col // 2 * parts
    slot = col % 2
    holds = (base <= ten) & (ten < base + parts)
    always = parts == n_tensor

    def guarded(condition, action):
        if always:
            action()
        else:
            pl.when(condition)(action)

    def w_part(k):
        index = (ten + k) % parts
        piece = w_ref.at[:, pl.ds(pl.multiple_of(index * width, width), width)]
        return piece, base + index

    def w_first(k):
        piece, target = w_part(k)
        return remote(piece, wbuf.at[slot, ten], w_send.at[k], w_recv.at[ten], seq, target)

    def w_keep():
        return pltpu.make_async_copy(w_part(0)[0], wbuf.at[slot, ten], w_local)

    def w_second(i, k):
        source = (ten + k) % n_tensor
        at = wbuf.at[slot, source]
        return remote(
            w_part(0)[0] if k == 0 else at,
            at,
            w_across.at[i, k],
            w_crossed.at[slot, source],
            col_peer(i),
            ten,
        )

    def w_begin():
        w_keep().start()
        for i in range(1, rest):
            w_second(i, 0).start()

    if not always:
        pl.when(jnp.logical_not(holds))(lambda: w_first(0).start())
    for k in range(1, parts):
        w_first(k).start()
    guarded(holds, w_begin)

    def kv_arrive(i, j, h):
        kv_copy(kv_source(i, j), h, i, j, seq).wait_recv()

    def kv_relay(i, h):
        kv_arrive(i, 2, h)
        kv_start(kv_source(i, 2), h, i, 3, line_peer(1))

    for h in range(2):
        kv_relay(0, h)
        for i in range(1, rest):
            kv_arrive(i, 0, h)
            kv_square(i, h)
    for h in range(2):
        for i in range(1, rest):
            kv_relay(i, h)

    def w_relay():
        for k in range(1, n_tensor):
            source = (ten + k) % n_tensor
            remote(
                w_part(0)[0], wbuf.at[slot, source], w_send.at[0], w_recv.at[source], seq, ten
            ).wait_recv()
            for i in range(1, rest):
                w_second(i, k).start()
        w_keep().wait()

    guarded(holds, w_relay)

    def w_wait(u):
        owner = ten // parts * 2 + u

        @pl.when(owner != col)
        def _():
            for k in range(n_tensor):
                at = wbuf.at[u, k]
                remote(at, at, w_across.at[0, 0], w_crossed.at[u, k], seq, ten).wait_recv()

    starts = [jnp.int32(0)]
    for p in range(n_prompts - 1):
        starts.append(starts[-1] + len_ref[p])

    def kv_wait(h):
        for i in range(rest):
            for j in (1, 3):
                kv_arrive(i, j, h)

    def att_at(h, at_line, at_ten):
        return att.at[at_line, at_ten, pl.ds(h * half, half)]

    def proj_at(u, at_line, at_ten):
        return proj.at[u, at_line, at_ten]

    def piece_copy(where, n, send, recv, at_line, at_ten, slot, to_ten):
        at = where(n, at_line, at_ten)
        return remote(at, at, send.at[(n,) + slot], recv.at[n, at_line, at_ten], seq, to_ten)

    def spread(where, n, send, recv, j):
        at_line = place(j)
        for i in range(1, pairs):
            copy = piece_copy(where, n, send, recv, at_line, ten, (j, i), pair_peer(i))
            copy.start()
            sent.append(copy)
        copy = piece_copy(where, n, send, recv, at_line, ten, (j, pairs), twin)
        copy.start()
        sent.append(copy)

    def relay(where, n, send, recv, j):
        at_line = place(j)
        for i in range(1, pairs):
            source = pair_peer(pairs - i)
            piece_copy(where, n, send, recv, at_line, source, (j, 0), ten).wait_recv()
            copy = piece_copy(where, n, send, recv, at_line, source, (j, pairs + i), twin)
            copy.start()
            sent.append(copy)

    def settle(where, n, send, recv, j):
        at_line = place(j)
        for y in range(pairs):
            source = y * CORES + 1 - core
            piece_copy(where, n, send, recv, at_line, source, (j, 0), ten).wait_recv()

    def arrive(where, n, send, recv, j):
        at_line = place(j)
        piece_copy(where, n, send, recv, at_line, ten, (j, 0), ten).wait_recv()
        spread(where, n, send, recv, j)

    def att_copy(h, j, y, slot, to_seq, to_ten):
        at_line, at_ten = place(j), pair_peer(y)
        at = att_at(h, at_line, at_ten)
        return remote(
            at, at, a_send.at[(h,) + slot], a_recv.at[h, at_line, at_ten], to_seq, to_ten
        )

    def att_send(h, j, y, slot, to_seq, to_ten):
        copy = att_copy(h, j, y, slot, to_seq, to_ten)
        copy.start()
        sent.append(copy)

    def att_round(h, y):
        for j in (2, 1):
            att_send(h, 0, y, (j, y), line_peer(j), ten)
        att_send(h, 0, y, (0, pairs + y), seq, twin)

    def att_arrive(h, j, y):
        att_copy(h, j, y, (0, 0), seq, ten).wait_recv()

    scale = math.log2(math.e) / math.sqrt(HD)
    for h in range(2):
        kv_wait(h)
        block = seq if h == 0 else 2 * n_seq - 1 - seq
        position = block * half + lax.broadcasted_iota(jnp.int32, (half, 1), 0)
        begin = jnp.zeros((half, 1), jnp.int32)
        for p in range(1, n_prompts):
            begin = jnp.where(starts[p] <= position, starts[p], begin)
        m_ref[...] = jnp.full_like(m_ref, -1e20)
        l_ref[...] = jnp.zeros_like(l_ref)
        acc_ref[...] = jnp.zeros_like(acc_ref)

        def step(c, carry, h=h, position=position, begin=begin):
            at = pl.ds(pl.multiple_of(c * KEYS, KEYS), KEYS)
            where = c * KEYS + lax.broadcasted_iota(jnp.int32, (half, KEYS), 1)
            bias = jnp.where((where >= begin) & (where <= position), 0.0, -1e30)
            for g in range(heads):
                scores = lax.dot_general(
                    q_ref[h * half : (h + 1) * half, g * HD : (g + 1) * HD],
                    kv[at, :HD],
                    (((1,), (1,)), ((), ())),
                    preferred_element_type=jnp.float32,
                )
                scores = scores * scale + bias
                old = m_ref[g]
                top = jnp.maximum(old, jnp.max(scores, axis=1, keepdims=True))
                shrink = jnp.exp2(old - top)
                weights = jnp.exp2(scores - jnp.concatenate([top] * (KEYS // HD), axis=1))
                l_ref[g] = l_ref[g] * shrink + jnp.sum(weights, axis=1, keepdims=True)
                acc_ref[g] = acc_ref[g] * shrink + jnp.dot(
                    weights.astype(jnp.bfloat16), kv[at, HD:], preferred_element_type=jnp.float32
                )
                m_ref[g] = top
            return carry

        lax.fori_loop(0, ((block + 1) * half + KEYS - 1) // KEYS, step, 0)
        for g in range(heads):
            att[line, ten, h * half : (h + 1) * half, g * HD : (g + 1) * HD] = (
                acc_ref[g] / l_ref[g]
            ).astype(jnp.bfloat16)
        for i in range(1, pairs):
            att_send(h, 0, 0, (0, i), seq, pair_peer(i))
        att_round(h, 0)

    def multiply(u, j):
        at_line = place(j)

        def add(k, total):
            return total + jnp.dot(
                att[at_line, k], wbuf[u, k], preferred_element_type=jnp.float32
            )

        total = lax.fori_loop(0, n_tensor, add, jnp.zeros((rows, width), jnp.float32))
        if j == 0:
            proj[u, line, ten] = total.astype(jnp.bfloat16)
            spread(proj_at, u, p_send, p_recv, 0)
        else:
            prod[u, j] = total.astype(jnp.bfloat16)
            copy = remote(
                prod.at[u, j],
                proj.at[u, line, ten],
                p_send.at[u, j, 0],
                p_recv.at[u, line, ten],
                line_peer(j),
                ten,
            )
            copy.start()
            sent.append(copy)

    square[...] = jnp.zeros_like(square)

    def column(u, a, t):
        place = ((t // parts * 2 + u) * LINE + a) * parts + t % parts
        return pl.ds(pl.multiple_of(place * width, width), width)

    def write(u, a, t):
        return pltpu.make_async_copy(
            proj.at[u, a, t], out_ref.at[:, column(u, a, t)], out_sem.at[u, a, t]
        )

    def collect(u, j):
        settle(proj_at, u, p_send, p_recv, j)
        at_line = place(j)

        def add(t, carry):
            write(u, at_line, t).start()
            hidden = res[:, column(u, at_line, t)].astype(jnp.float32) + proj[
                u, at_line, t
            ].astype(jnp.float32)
            power = hidden * hidden
            for part in range(width // HD):
                square[...] += power[:, part * HD : (part + 1) * HD]
            return carry

        lax.fori_loop(0, n_tensor, add, 0)

    order = (0, 2, 1, 3)
    other = 1 - slot
    w_wait(slot)
    for h in range(2):
        for y in range(1, pairs):
            att_arrive(h, 0, y)
            att_round(h, y)
    for n in range(LINE):
        for h in range(2):
            for y in range(pairs):
                if n > 0:
                    att_arrive(h, order[n], y)
                    if order[n] == 2:
                        att_send(h, 2, y, (3, y), line_peer(1), ten)
                    att_send(h, order[n], y, (order[n], pairs + y), seq, twin)
        for h in range(2):
            settle(att_at, h, a_send, a_recv, order[n])
        multiply(slot, order[n])
    for n in range(1, LINE):
        arrive(proj_at, slot, p_send, p_recv, order[n])

    slots = seq * SLOT_DEV + lax.broadcasted_iota(jnp.int32, (SLOT_DEV, 1), 0)
    source_of = jnp.full((SLOT_DEV, 1), -1, jnp.int32)
    page = jnp.int32(0)
    for p in range(n_prompts):
        length = len_ref[p]
        within = slots - page
        live = (within >= 0) & (within < length)
        source_of = jnp.where(live, within + starts[p], source_of)
        page = page + (length + PAGE - 1) // PAGE * PAGE
    picked = jnp.zeros((SLOT_DEV, 2 * HD), jnp.float32)

    def pick(c, picked):
        at = pl.ds(pl.multiple_of(c * KEYS, KEYS), KEYS)
        where = c * KEYS + lax.broadcasted_iota(jnp.int32, (SLOT_DEV, KEYS), 1)
        hot = jnp.where(where == source_of, 1.0, 0.0).astype(jnp.bfloat16)
        return picked + jnp.dot(hot, kv[at, :], preferred_element_type=jnp.float32)

    picked = lax.fori_loop(0, tokens // KEYS, pick, picked)
    ck_ref[...] = picked[:, :HD].astype(jnp.bfloat16)
    cv_ref[...] = picked[:, HD:].astype(jnp.bfloat16)

    w_wait(other)
    res_copy.wait()
    for n in range(LINE):
        multiply(other, order[n])
    for n in range(LINE):
        if n + 1 < LINE:
            arrive(proj_at, other, p_send, p_recv, order[n + 1])
        relay(proj_at, slot, p_send, p_recv, order[n])
    for n in range(LINE):
        collect(slot, order[n])
        relay(proj_at, other, p_send, p_recv, order[n])
    for n in range(LINE):
        collect(other, order[n])
    total = jnp.sum(square[...], axis=1, keepdims=True)
    factor = lax.rsqrt(total * (1.0 / res.shape[1]) + 1e-05)
    factor_ref[...] = jnp.broadcast_to(factor, factor_ref.shape)
    for u in range(2):
        for a in range(LINE):
            for t in range(n_tensor):
                write(u, a, t).wait()

    for copy in sent:
        copy.wait_send()
    for k in range(1, parts):
        w_first(k).wait_send()
    if not always:
        pl.when(jnp.logical_not(holds))(lambda: w_first(0).wait_send())

    def w_sent():
        for i in range(1, rest):
            for k in range(n_tensor):
                w_second(i, k).wait_send()

    guarded(holds, w_sent)


def body(
    n_seq, n_tensor, queries, key_rows, value_rows, out_weight, residual_in, norm_gain, lengths
):
    rows, model = residual_in.shape
    width = model // (LINE * n_tensor) // 2
    rest, pairs = n_seq // LINE, n_tensor // CORES
    parts = out_weight.shape[1] // width
    half = rows // 2
    heads = queries.shape[1] // HD
    depth = out_weight.shape[0]
    vmem = pl.BlockSpec(memory_space=pltpu.VMEM)
    hbm = pl.BlockSpec(memory_space=pl.ANY)
    dma = pltpu.SemaphoreType.DMA
    projected, factor, cache_keys, cache_values = pl.pallas_call(
        functools.partial(kernel, n_seq, n_tensor),
        out_shape=(
            jax.ShapeDtypeStruct((rows, model), jnp.bfloat16),
            jax.ShapeDtypeStruct((rows, HD), jnp.float32),
            jax.ShapeDtypeStruct((SLOT_DEV, HD), jnp.bfloat16),
            jax.ShapeDtypeStruct((SLOT_DEV, HD), jnp.bfloat16),
        ),
        in_specs=[vmem, vmem, vmem, hbm, hbm, pl.BlockSpec(memory_space=pltpu.SMEM)],
        out_specs=(hbm, vmem, vmem, vmem),
        scratch_shapes=[
            pltpu.VMEM((rows * n_seq, 2 * HD), jnp.bfloat16),
            pltpu.VMEM((2, n_tensor, depth, width), jnp.bfloat16),
            pltpu.VMEM((LINE, n_tensor, rows, depth), jnp.bfloat16),
            pltpu.VMEM((2, LINE, rows, width), jnp.bfloat16),
            pltpu.VMEM((2, LINE, n_tensor, rows, width), jnp.bfloat16),
            pltpu.VMEM((rows, model), jnp.bfloat16),
            pltpu.VMEM((heads, half, HD), jnp.float32),
            pltpu.VMEM((heads, half, HD), jnp.float32),
            pltpu.VMEM((heads, half, HD), jnp.float32),
            pltpu.VMEM((rows, HD), jnp.float32),
            dma((rest, LINE, 2)),
            dma((n_seq, 2)),
            dma((parts,)),
            dma((n_tensor,)),
            dma,
            dma((rest, n_tensor)),
            dma((2, n_tensor)),
            dma((2, LINE, 2 * pairs)),
            dma((2, LINE, n_tensor)),
            dma((2, LINE, 2 * pairs)),
            dma((2, LINE, n_tensor)),
            dma,
            dma((2, LINE, n_tensor)),
        ],
        compiler_params=pltpu.CompilerParams(
            collective_id=0, has_side_effects=True, vmem_limit_bytes=58 * 2**20
        ),
        cost_estimate=pl.CostEstimate(
            flops=5 * 10**9, bytes_accessed=14 * 10**6, transcendentals=2 * 10**6
        ),
    )(
        queries,
        key_rows,
        value_rows,
        out_weight,
        residual_in,
        lengths,
    )
    hidden = residual_in.astype(jnp.float32) + projected.astype(jnp.float32)
    normed = hidden * factor[:, :1] * norm_gain.astype(jnp.float32)
    return normed.astype(jnp.bfloat16), cache_keys, cache_values


def solution(mesh):
    return jax.shard_map(
        functools.partial(body, mesh.shape["seq"], mesh.shape["tensor"]),
        mesh=mesh,
        in_specs=(
            P("seq", "tensor"),
            P("seq", "tensor"),
            P("seq", "tensor"),
            P("tensor", "seq"),
            P("seq", None),
            P(),
            P(),
        ),
        out_specs=(P("seq", None), P("seq", "tensor"), P("seq", "tensor")),
        check_vma=False,
    )
```
